128 devices in a mesh: row: 8 (over x, core), col: 16 (over z, y).
Axes of the slice: x: 4, y: 4, z: 4, core: 2. Of those that a mesh axis runs over, the one named last changes fastest.
Arguments:
- coords: float32 [4, 16384], P(None, ('row', 'col')), may hold values from 0 to 1, as said below
- values: float32 [512, 16384], P(None, ('row', 'col')), may hold values from -6 to 6
- coarse_coords: float32 [4, 2048], P(None, ('row', 'col')), may hold values from 0 to 1, as said below
- coarse_values: float32 [512, 2048], P(None, ('row', 'col')), may hold values from -6 to 6
- fine_index: int32 [128, 128], P(('row', 'col')), may hold values from 0 to 127, as said below
- coarse_index: int32 [128, 384], P(('row', 'col')), may hold values from 0 to 2047, as said below
- log_params: float32 [6], replicated, may hold values from -0.5 to 0.5
Outputs:
- step: float32 [6], replicated
- whitened: float32 [512, 16384], P(None, ('row', 'col'))
The draws below stay inside these ranges and needn't reach their ends.
Inputs may be any that keep to these rules, and one draw needn't show every extreme that they name: `fine_index`: in each row the first 64 entries are distinct, and so are the last 64. `coarse_index`: the entries of each row are distinct; in each row at most 6 entries lie in one tile (j // 16), and some tile holds exactly 6 of them. `coarse_coords`: coarse point j lies in tile j // 16; for tile (r, c) its longitude lies in [c / 16, (c + 1) / 16) and its latitude in [r / 8, (r + 1) / 8), elevation and time in [0, 1). `coords`: fine point p lies in tile p // 128, placed as for the coarse points.
All inputs are finite; a program needn't handle non-finite values.
Results may differ from the reference program's by a relative error of at most 0.0003.
Values sent between devices are 32-bit elements; how exact they have to be, the bound alone decides.
No kernel may reach another device: no remote copies, remote signals or barrier semaphores. Data moves between devices by JAX's collectives and lax.ppermute only.
A program may use at most 192 MiB of HBM per device.

```python
import math
import jax
import jax.numpy as jnp
from jax import lax

R = 512
B = 128
FH = 64
COARSE = 384
CP = 16
TOTAL = 16384
CTOTAL = 2048
N_ROW = 8
N_COL = 16
DEVICES = 128


def placed_coords(key, per_tile):
    count = DEVICES * per_tile
    unit = jax.random.uniform(key, (4, count), jnp.float32)
    owner = jnp.arange(count, dtype=jnp.int32) // per_tile
    col_pos = (owner % N_COL).astype(jnp.float32)
    row_pos = (owner // N_COL).astype(jnp.float32)
    longitude = (col_pos + unit[0]) / float(N_COL)
    latitude = (row_pos + unit[1]) / float(N_ROW)
    return jnp.stack([longitude, latitude, unit[2], unit[3]])


def draw_coords(key, part):
    return placed_coords(jax.random.fold_in(key, 11), B)


def draw_coarse_coords(key, part):
    return placed_coords(jax.random.fold_in(key, 13), CP)


def draw_fine_index(key, part):
    keys = jax.random.split(jax.random.fold_in(key, 17), 2 * DEVICES)
    picks = jax.vmap(lambda each: jax.random.permutation(each, B)[:FH])(keys)
    return picks.reshape(DEVICES, 2 * FH).astype(jnp.int32)


def one_coarse_row(each):
    limit = min(CP, 2 * ((COARSE + DEVICES - 1) // DEVICES))
    first_key, second_key, third_key = jax.random.split(each, 3)
    forced = jax.random.randint(first_key, (), 0, DEVICES, dtype=jnp.int32)
    pairs = DEVICES * limit
    ranks = jax.random.permutation(second_key, pairs).astype(jnp.int32)
    tile_of = jnp.arange(pairs, dtype=jnp.int32) // limit
    scores = jnp.where(tile_of == forced, ranks - pairs, ranks)
    chosen = jnp.argsort(scores, stable=True)[:COARSE].astype(jnp.int32)
    chosen_tile = chosen // limit
    chosen_slot = chosen % limit
    sub_keys = jax.random.split(third_key, DEVICES)
    inner = jax.vmap(lambda sub: jax.random.permutation(sub, CP))(sub_keys).astype(jnp.int32)
    return chosen_tile * CP + inner[chosen_tile, chosen_slot]


def draw_coarse_index(key, part):
    keys = jax.random.split(jax.random.fold_in(key, 19), DEVICES)
    return jax.vmap(one_coarse_row)(keys).astype(jnp.int32)


def block_scale(rng, dims, pieces, low, top_value):
    def one(dim, blocks):
        steps = jax.random.uniform(jax.random.fold_in(jax.random.fold_in(rng, 6), dim), (blocks,), jnp.float32, low / len(pieces), top_value / len(pieces))
        return jnp.repeat(jnp.exp(steps), dims[dim] // blocks).reshape((-1,) + (1,) * (len(dims) - dim - 1))

    level = one(*pieces[0])
    for cut in pieces[1:]:
        level = level * one(*cut)
    return level


def normal_values(key, shape, deviation, bound, pieces=(), kind=jnp.bfloat16):
    values = deviation * jax.random.normal(key, shape, jnp.float32)
    if pieces:
        values = values * block_scale(key, shape, pieces, -0.22, 0.18)
    return jnp.clip(values, -bound, bound).astype(kind)


def setup_inputs(seed: int = 0) -> dict:
    key_of = jax.random.split(jax.random.key(seed), 8)
    coords = draw_coords(jax.random.fold_in(key_of[7], 71), 0)
    values = normal_values(key_of[1], (R, TOTAL), 1.0, 6.0, ((1, 128),), jnp.float32)
    coarse_coords = draw_coarse_coords(jax.random.fold_in(key_of[7], 71), 0)
    coarse_values = normal_values(key_of[3], (R, CTOTAL), 1.0, 6.0, ((1, 128),), jnp.float32)
    fine_index = draw_fine_index(jax.random.fold_in(key_of[7], 71), 0)
    coarse_index = draw_coarse_index(jax.random.fold_in(key_of[7], 71), 0)
    log_params = jnp.clip(jax.random.uniform(key_of[6], (6,), jnp.float32, -0.5, 0.5), -0.5, 0.5)
    return dict(coords=coords, values=values, coarse_coords=coarse_coords, coarse_values=coarse_values, fine_index=fine_index, coarse_index=coarse_index, log_params=log_params)


HIGH = lax.Precision.HIGHEST
ROOT_FIVE = math.sqrt(5.0)
NUGGET = 0.2
RANGE_BASE = (0.5, 0.5, 0.5, 0.5)

def local_covariance(joint_coords, live, theta):
    count = joint_coords.shape[1]
    scale = jnp.exp(theta[1:5]) * jnp.array(RANGE_BASE)
    scaled = joint_coords / scale[:, None]
    diff = scaled[:, :, None] - scaled[:, None, :]
    squares = diff * diff
    dist = jnp.sqrt(lax.optimization_barrier(jnp.sum(squares, axis=0)))
    root = ROOT_FIVE * dist
    decay = jnp.exp(-root)
    variance = jnp.exp(theta[0])
    kernel = variance * (1.0 + root + root * root / 3.0) * decay
    common = variance * (5.0 / 3.0) * (1.0 + root) * decay
    paired = live[:, None] * live[None, :]
    ident = jnp.eye(count, dtype=jnp.float32)
    nugget = NUGGET * jnp.exp(theta[5])
    cov = paired * kernel + (live * nugget + 1.0 - live)[:, None] * ident
    derivs = jnp.concatenate([(paired * kernel)[None], (paired * common)[None] * squares, ((live * nugget)[:, None] * ident)[None]], axis=0)
    return (cov, derivs)

def fisher_terms(cov, derivs, lead, reps):
    count = cov.shape[0]
    ident = jnp.eye(count, dtype=jnp.float32)
    factor = jnp.linalg.cholesky(cov)
    inverse = jax.scipy.linalg.solve_triangular(factor, ident, lower=True)
    joint_prec = jnp.dot(inverse.T, inverse, precision=HIGH)
    lead_inv = inverse[:lead, :lead]
    lead_prec = jnp.dot(lead_inv.T, lead_inv, precision=HIGH)
    joint_prod = jnp.einsum('ab,ibc->iac', joint_prec, derivs, precision=HIGH)
    lead_prod = jnp.einsum('ab,ibc->iac', lead_prec, derivs[:, :lead, :lead], precision=HIGH)
    joint_fish = jnp.einsum('iab,jba->ij', joint_prod, joint_prod, precision=HIGH)
    lead_fish = jnp.einsum('iab,jba->ij', lead_prod, lead_prod, precision=HIGH)
    fisher = reps * 0.5 * (joint_fish - lead_fish)
    traces = jnp.trace(joint_prod, axis1=1, axis2=2) - jnp.trace(lead_prod, axis1=1, axis2=2)
    return (inverse, fisher, traces)

def score_terms(inverse, derivs, joint_values, traces, lead, reps):
    white = jnp.dot(joint_values, inverse.T, precision=HIGH)
    alpha = jnp.dot(white, inverse, precision=HIGH)
    lead_alpha = jnp.dot(white[:, :lead], inverse[:lead, :lead], precision=HIGH)
    joint_quad = lax.optimization_barrier(jnp.sum(jnp.einsum('rn,inm->irm', alpha, derivs, precision=HIGH) * alpha[None], axis=(1, 2)))
    lead_quad = lax.optimization_barrier(jnp.sum(jnp.einsum('rn,inm->irm', lead_alpha, derivs[:, :lead, :lead], precision=HIGH) * lead_alpha[None], axis=(1, 2)))
    grad = 0.5 * (joint_quad - lead_quad) - 0.5 * reps * traces
    return (grad, white[:, lead:])

def reference(coords, values, coarse_coords, coarse_values, fine_index, coarse_index, log_params):
    lead = COARSE + 2 * FH
    tile_coords = coords.reshape(4, DEVICES, B)
    tile_values = values.reshape(R, DEVICES, B)

    def one_block(device):
        row_pos = device // N_COL
        col_pos = device % N_COL
        upper = jnp.maximum(device - N_COL, 0).astype(jnp.int32)
        left = (row_pos * N_COL + (col_pos + N_COL - 1) % N_COL).astype(jnp.int32)
        upper_live = (row_pos > 0).astype(jnp.float32)
        picks = fine_index[device]
        wanted = coarse_index[device]
        upper_coords = jnp.take(jnp.take(tile_coords, upper, axis=1), picks[:FH], axis=1) * upper_live
        upper_values = jnp.take(jnp.take(tile_values, upper, axis=1), picks[:FH], axis=1) * upper_live
        left_coords = jnp.take(jnp.take(tile_coords, left, axis=1), picks[FH:], axis=1)
        left_values = jnp.take(jnp.take(tile_values, left, axis=1), picks[FH:], axis=1)
        joint_coords = jnp.concatenate([jnp.take(coarse_coords, wanted, axis=1), upper_coords, left_coords, jnp.take(tile_coords, device, axis=1)], axis=1)
        joint_values = jnp.concatenate([jnp.take(coarse_values, wanted, axis=1), upper_values, left_values, jnp.take(tile_values, device, axis=1)], axis=1)
        live = jnp.concatenate([jnp.ones((COARSE,), jnp.float32), upper_live * jnp.ones((FH,), jnp.float32), jnp.ones((FH + B,), jnp.float32)])
        cov, derivs = local_covariance(joint_coords, live, log_params)
        inverse, fisher, traces = fisher_terms(cov, derivs, lead, R)
        grad, white = score_terms(inverse, derivs, joint_values, traces, lead, R)
        return (grad, fisher, white)
    grads, fishers, whites = lax.map(one_block, jnp.arange(DEVICES, dtype=jnp.int32))
    grad = lax.optimization_barrier(jnp.sum(grads, axis=0))
    fisher = lax.optimization_barrier(jnp.sum(fishers, axis=0))
    step = jax.scipy.linalg.cho_solve((jnp.linalg.cholesky(fisher), True), grad)
    whitened = jnp.transpose(whites, (1, 0, 2)).reshape(R, DEVICES * B)
    return (step, whitened)
```

```python
import math

import jax
import jax.numpy as jnp
from jax import lax
from jax.experimental import pallas as pl
from jax.experimental.pallas import tpu as pltpu
from jax.sharding import PartitionSpec as P

HIGH = lax.Precision.HIGHEST
ROOT_FIVE = math.sqrt(5.0)
NUGGET = 0.2
RANGE_BASE = 0.5
F32 = jnp.float32
BF16 = jnp.bfloat16
AXES = ("row", "col")

B = 128
N = 640
LEAD = 512
COARSE = 384
HALF = 64
CP = 16
GROUP = 8


def shifted(value, axis, steps):
    count = lax.axis_size(axis)
    first, last = (max(0, -steps), min(count, count - steps))
    return lax.ppermute(value, axis, [(source, source + steps) for source in range(first, last)])


def passed_along(block, axis, distance):
    devices = range(lax.axis_size(axis))
    route = [((i - distance) % len(devices), i) for i in devices]
    return lax.ppermute(block, axis, route)


def nn(a, b, precision=HIGH):
    return lax.dot_general(a, b, (((1,), (0,)), ((), ())), precision=precision, preferred_element_type=F32)


def nt(a, b, precision=HIGH):
    return lax.dot_general(a, b, (((1,), (1,)), ((), ())), precision=precision, preferred_element_type=F32)


def tn(a, b, precision=HIGH):
    return lax.dot_general(a, b, (((0,), (0,)), ((), ())), precision=precision, preferred_element_type=F32)


def iota(shape, dim):
    return lax.broadcasted_iota(jnp.int32, shape, dim)


def halves(x):
    high = x.astype(BF16)
    return high, (x - high.astype(F32)).astype(BF16)


def thirds(x):
    high = x.astype(BF16)
    rest = x - high.astype(F32)
    mid = rest.astype(BF16)
    return high, mid, (rest - mid.astype(F32)).astype(BF16)


def picked(table, one_hot, dot):
    high, mid, low = thirds(table)
    return (dot(high, one_hot, None) + dot(mid, one_hot, None)) + dot(low, one_hot, None)


def inverse_factor(s):
    tiles = B // 8
    s = list(s)
    sub, lane = iota((8, B), 0), iota((8, B), 1)
    scale = [jnp.zeros((8, B), F32)] * tiles
    for k0 in range(0, B, GROUP):
        v0 = k0 // 8
        live = range(v0, tiles)
        cols = [{v: jnp.broadcast_to(s[v][:, j : j + 1], (8, B)) for v in live} for j in range(k0, k0 + GROUP)]
        inside = (lane >= k0) & (lane < k0 + GROUP)
        s[v0] = jnp.where(inside, (lane == sub + 8 * v0).astype(F32), s[v0])
        for v in range(v0 + 1, tiles):
            s[v] = jnp.where(inside, 0.0, s[v])
        for j in range(GROUP):
            k = (k0 + j) % 8
            col = cols[j]
            pivot = jnp.broadcast_to(col[v0][k : k + 1, :], (8, B))
            scale[v0] = jnp.where(sub == k, pivot, scale[v0])
            over = 1.0 / pivot
            factor = {v: col[v] * over for v in live}
            factor[v0] = jnp.where(sub > k, factor[v0], 0.0)
            for later in range(j + 1, GROUP):
                at = jnp.broadcast_to(cols[later][v0][k : k + 1, :], (8, B))
                for v in live:
                    cols[later][v] = cols[later][v] - factor[v] * at
            row = jnp.broadcast_to(s[v0][k : k + 1, :], (8, B))
            for v in live:
                s[v] = s[v] - factor[v] * row
    out = []
    for v in range(tiles):
        root = lax.rsqrt(scale[v])
        root = root * (1.5 - 0.5 * scale[v] * root * root)
        out.append(jnp.where(lane <= sub + 8 * v, s[v] * root, 0.0))
    return out


def first_kernel(theta, table, up, left, own, fine, coarse, m_ref, z_ref, g_ref, part_ref, k_ref, d_ref, u_ref, f_ref, y_ref):
    tile_hot = (iota((B, COARSE), 0) == coarse[...] // CP).astype(BF16)
    rows = picked(table[...], tile_hot, tn)
    slot = coarse[...] % CP
    wanted = (iota((4 * CP, COARSE), 0) % CP) == slot
    rows = jnp.where(wanted, rows, 0.0)
    coarse_rows = [jnp.sum(rows[k * CP : (k + 1) * CP], axis=0, keepdims=True) for k in range(4)]
    up_hot = (iota((B, HALF), 0) == fine[:, :HALF]).astype(BF16)
    left_hot = (iota((B, HALF), 0) == fine[:, HALF:]).astype(BF16)
    up_rows = picked(up[...], up_hot, nn)
    left_rows = picked(left[...], left_hot, nn)
    upper_live = (lax.axis_index("row") > 0).astype(F32)
    lane = iota((1, N), 1)
    live = jnp.where((lane >= COARSE) & (lane < COARSE + HALF), upper_live, 1.0)
    across = []
    for k in range(4):
        line = jnp.concatenate(
            [coarse_rows[k], up_rows[k : k + 1] * upper_live, left_rows[k : k + 1], own[k : k + 1, :]], axis=1
        )
        across.append(line / (jnp.exp(jnp.full((1, N), theta[1 + k], F32)) * RANGE_BASE))
    down = jnp.concatenate(across + [live] + [jnp.zeros((B - 5, N), F32)], axis=0).T
    variance = jnp.exp(jnp.full((1, N), theta[0], F32))
    nugget = NUGGET * jnp.exp(jnp.full((1, N), theta[5], F32))
    for r in range(N // B):
        here = slice(r * B, (r + 1) * B)
        squares = []
        for k in range(4):
            gap = down[here, k : k + 1] - across[k]
            squares.append(gap * gap)
        root = ROOT_FIVE * jnp.sqrt((squares[0] + squares[1]) + (squares[2] + squares[3]))
        decay = jnp.exp(-root)
        paired = (down[here, 4:5] * live) * (variance * decay)
        kernel = paired * (1.0 + root + root * root * (1.0 / 3.0))
        common = paired * ((5.0 / 3.0) * (1.0 + root))
        f_ref[0, here, :] = kernel
        for k in range(4):
            f_ref[1 + k, here, :] = common * squares[k]
        same = iota((B, N), 0) + r * B == iota((B, N), 1)
        k_ref[here, :] = kernel + jnp.where(same, live * nugget + 1.0 - live, 0.0)

    def sweep(p, carry):
        at = pl.multiple_of(p * B, B)
        tiles = inverse_factor([k_ref[pl.ds(at + 8 * v, 8), pl.ds(at, B)] for v in range(B // 8)])
        for v in range(B // 8):
            d_ref[8 * v : 8 * (v + 1), :] = tiles[v]

        @pl.when(p < N // B - 1)
        def _():
            d = d_ref[...]
            u_ref[...] = nn(d, k_ref[pl.ds(at, B), :])
            u_ref[:, pl.ds(at, B)] = -d
            k_ref[pl.ds(at, B), :] = jnp.zeros((B, N), F32)
            k_ref[:, pl.ds(at, B)] = jnp.zeros((N, B), F32)
            k_ref[...] -= tn(u_ref[...], u_ref[...])

        return carry

    lax.fori_loop(0, N // B, sweep, 0)
    d = d_ref[...]
    m_ref[:, :LEAD] = -nt(d, k_ref[:LEAD, LEAD:])
    m_ref[:, LEAD:] = d
    m = m_ref[...]
    for i in range(5):
        y_ref[i * B : (i + 1) * B, :] = nn(m, f_ref[i])
    y_ref[5 * B :, :] = m * (live * nugget)
    z_ref[...] = -nn(y_ref[:, :LEAD], k_ref[:LEAD, :LEAD])
    g_ref[...] = nt(y_ref[...], m)

    def folded(x):
        x = jnp.sum(x.reshape(B // 8, 8, x.shape[1]), axis=0)
        total = x[:, :B]
        for c in range(1, x.shape[1] // B):
            total = total + x[:, c * B : (c + 1) * B]
        return total

    sums = []
    for i in range(6):
        for j in range(i + 1):
            lead_part = z_ref[i * B : (i + 1) * B, :] * y_ref[j * B : (j + 1) * B, :LEAD]
            own_part = g_ref[i * B : (i + 1) * B, :] * g_ref[j * B : (j + 1) * B, :]
            sums.append(jnp.sum(2.0 * folded(lead_part) + folded(own_part), axis=0, keepdims=True))
    for i in range(6):
        sums.append(jnp.sum(folded(y_ref[i * B : (i + 1) * B, :] * m), axis=0, keepdims=True))
    sums.append(jnp.zeros((5, B), F32))
    part_ref[...] = jnp.concatenate(sums, axis=0)


def second_kernel(every, up, left, own, fine, coarse, m, z, g, part, white_ref, row_ref, v_ref):
    reps = own.shape[0]
    down = jnp.concatenate([coarse[...], fine[...], jnp.zeros((1, B), jnp.int32)], axis=1)
    down = jnp.broadcast_to(down.astype(F32), (B, N)).T.astype(jnp.int32)[:, :1]
    hot = (down[:COARSE] == iota((COARSE, every.shape[0]), 1)).astype(BF16)
    high, low = halves(every[...])
    v_ref[:COARSE, :] = nn(hot, high, None) + nn(hot, low, None)
    hot = (down[COARSE:LEAD] == iota((B, B), 1)).astype(BF16)
    v_ref[COARSE : COARSE + HALF, :] = picked2(hot[:HALF], up[...])
    v_ref[COARSE + HALF : LEAD, :] = picked2(hot[HALF:], left[...])
    v_ref[LEAD:, :] = own[...].T
    white = nn(m[...], v_ref[...])
    white_ref[...] = white.T
    cross = nt(white, v_ref[:LEAD, :])
    square = nt(white, white)
    lines = []
    eye = (iota((B, B), 0) == iota((B, B), 1)).astype(F32)
    for i in range(6):
        gi = g[i * B : (i + 1) * B, :]
        both = z[i * B : (i + 1) * B, :] * cross
        both = (both[:, :B] + both[:, B : 2 * B]) + (both[:, 2 * B : 3 * B] + both[:, 3 * B :])
        lines.append(jnp.sum(both + 0.5 * (gi * square), axis=0, keepdims=True) - (0.5 * reps) * part[21 + i : 22 + i, :])
    del eye
    whole = jnp.concatenate([(0.5 * reps) * part[:21, :]] + lines + [jnp.zeros((B - 27, B), F32)], axis=0)
    row_ref[...] = jnp.sum(whole.T, axis=0, keepdims=True)


def picked2(one_hot, table):
    high, low = halves(table)
    return nt(one_hot, high, None) + nt(one_hot, low, None)


def third_kernel(rows, step_ref):
    total = jnp.broadcast_to(jnp.sum(rows[...], axis=0, keepdims=True), (8, B))
    sub, lane = iota((8, B), 0), iota((8, B), 1)
    a = jnp.zeros((8, B), F32)
    for i in range(6):
        for j in range(6):
            low, high = min(i, j), max(i, j)
            entry = jnp.broadcast_to(total[:, high * (high + 1) // 2 + low : high * (high + 1) // 2 + low + 1], (8, B))
            a = jnp.where((sub == i) & (lane == j), entry, a)
        entry = jnp.broadcast_to(total[:, 21 + i : 22 + i], (8, B))
        a = jnp.where((sub == i) & (lane == 6), entry, a)
    for k in range(6):
        row = jnp.broadcast_to(a[k : k + 1, :], (8, B))
        col = jnp.broadcast_to(a[:, k : k + 1], (8, B))
        row = row / jnp.broadcast_to(row[:, k : k + 1], (8, B))
        a = jnp.where(sub == k, row, a - col * row)
    step_ref[...] = a


def body(coords, values, coarse_coords, coarse_values, fine_index, coarse_index, log_params):
    reps = values.shape[0]
    devices = lax.axis_size("row") * lax.axis_size("col")
    every = lax.all_gather(coarse_values.T, AXES, axis=0, tiled=True)
    up_coords = shifted(coords, "row", 1)
    left_coords = passed_along(coords, "col", 1)
    up_values = shifted(values, "row", 1)
    left_values = passed_along(values, "col", 1)
    table = lax.all_to_all(
        jnp.broadcast_to(coarse_coords.reshape(1, 4 * CP), (devices, 4 * CP)), AXES, 0, 0, tiled=True
    )
    vmem = pl.BlockSpec(memory_space=pltpu.VMEM)
    smem = pl.BlockSpec(memory_space=pltpu.SMEM)
    m, z, g, part = pl.pallas_call(
        first_kernel,
        out_shape=(
            jax.ShapeDtypeStruct((B, N), F32),
            jax.ShapeDtypeStruct((6 * B, LEAD), F32),
            jax.ShapeDtypeStruct((6 * B, B), F32),
            jax.ShapeDtypeStruct((32, B), F32),
        ),
        in_specs=[smem] + [vmem] * 6,
        out_specs=(vmem,) * 4,
        scratch_shapes=[
            pltpu.VMEM((N, N), F32),
            pltpu.VMEM((B, B), F32),
            pltpu.VMEM((B, N), F32),
            pltpu.VMEM((5, N, N), F32),
            pltpu.VMEM((6 * B, N), F32),
        ],
        compiler_params=pltpu.CompilerParams(vmem_limit_bytes=40 * 2**20),
        name="fisher_part",
    )(log_params, table, up_coords, left_coords, coords, fine_index, coarse_index)
    white, row = pl.pallas_call(
        second_kernel,
        out_shape=(jax.ShapeDtypeStruct((reps, B), F32), jax.ShapeDtypeStruct((1, B), F32)),
        in_specs=[vmem] * 10,
        out_specs=(vmem,) * 2,
        scratch_shapes=[pltpu.VMEM((N, reps), F32)],
        compiler_params=pltpu.CompilerParams(vmem_limit_bytes=40 * 2**20),
        name="gradient_part",
    )(every, up_values, left_values, values, fine_index, coarse_index, m, z, g, part)
    rows = lax.all_to_all(jnp.broadcast_to(row, (devices, B)), AXES, 0, 0, tiled=True)
    step = pl.pallas_call(
        third_kernel,
        out_shape=jax.ShapeDtypeStruct((8, B), F32),
        in_specs=[vmem],
        out_specs=vmem,
        name="solve_part",
    )(rows)
    return (step[:6, 6], white)


def solution(mesh):
    in_specs = (
        P(None, AXES),
        P(None, AXES),
        P(None, AXES),
        P(None, AXES),
        P(AXES, None),
        P(AXES, None),
        P(),
    )
    out_specs = (P(), P(None, AXES))
    return jax.shard_map(body, mesh=mesh, in_specs=in_specs, out_specs=out_specs, check_vma=False)
```

```python
import math

import jax
import jax.numpy as jnp
from jax import lax
from jax.experimental import pallas as pl
from jax.experimental.pallas import tpu as pltpu
from jax.sharding import PartitionSpec as P

HIGH = lax.Precision.HIGHEST
ROOT_FIVE = math.sqrt(5.0)
NUGGET = 0.2
RANGE_BASE = 0.5
F32 = jnp.float32
BF16 = jnp.bfloat16
AXES = ("row", "col")

B = 128
N = 640
LEAD = 512
COARSE = 384
HALF = 64
CP = 16
MOST = 6
GROUP = 8


def shifted(value, axis, steps):
    count = lax.axis_size(axis)
    first, last = (max(0, -steps), min(count, count - steps))
    return lax.ppermute(value, axis, [(source, source + steps) for source in range(first, last)])


def passed_along(block, axis, distance):
    devices = range(lax.axis_size(axis))
    route = [((i - distance) % len(devices), i) for i in devices]
    return lax.ppermute(block, axis, route)


def nn(a, b, precision=HIGH):
    return lax.dot_general(a, b, (((1,), (0,)), ((), ())), precision=precision, preferred_element_type=F32)


def nt(a, b, precision=HIGH):
    return lax.dot_general(a, b, (((1,), (1,)), ((), ())), precision=precision, preferred_element_type=F32)


def tn(a, b, precision=HIGH):
    return lax.dot_general(a, b, (((0,), (0,)), ((), ())), precision=precision, preferred_element_type=F32)


def iota(shape, dim):
    return lax.broadcasted_iota(jnp.int32, shape, dim)


def halves(x):
    high = x.astype(BF16)
    return high, (x - high.astype(F32)).astype(BF16)


def thirds(x):
    high = x.astype(BF16)
    rest = x - high.astype(F32)
    mid = rest.astype(BF16)
    return high, mid, (rest - mid.astype(F32)).astype(BF16)


def picked(table, one_hot, dot):
    high, mid, low = thirds(table)
    return (dot(high, one_hot, None) + dot(mid, one_hot, None)) + dot(low, one_hot, None)


def six_left(x):
    one, two, three = thirds(x)
    return jnp.concatenate([one, one, two, two, one, three], axis=1)


def six_right(x):
    one, two, three = thirds(x)
    return jnp.concatenate([one, two, one, two, three, one], axis=0)


def three_terms(left, right, dot):
    rows = left[0].shape[0]
    both = dot(jnp.concatenate(left, axis=0), right[0], None)
    return (both[:rows] + both[rows:]) + dot(left[0], right[1], None)


def inverse_factor(s):
    tiles = B // 8
    s = list(s)
    sub, lane = iota((8, B), 0), iota((8, B), 1)
    scale = [jnp.zeros((8, B), F32)] * tiles
    for k0 in range(0, B, GROUP):
        v0 = k0 // 8
        live = range(v0, tiles)
        cols = [{v: jnp.broadcast_to(s[v][:, j : j + 1], (8, B)) for v in live} for j in range(k0, k0 + GROUP)]
        inside = (lane >= k0) & (lane < k0 + GROUP)
        s[v0] = jnp.where(inside, (lane == sub + 8 * v0).astype(F32), s[v0])
        for v in range(v0 + 1, tiles):
            s[v] = jnp.where(inside, 0.0, s[v])
        for j in range(GROUP):
            k = (k0 + j) % 8
            col = cols[j]
            pivot = jnp.broadcast_to(col[v0][k : k + 1, :], (8, B))
            scale[v0] = jnp.where(sub == k, pivot, scale[v0])
            over = 1.0 / pivot
            factor = {v: col[v] * over for v in live}
            factor[v0] = jnp.where(sub > k, factor[v0], 0.0)
            for later in range(j + 1, GROUP):
                at = jnp.broadcast_to(cols[later][v0][k : k + 1, :], (8, B))
                for v in live:
                    cols[later][v] = cols[later][v] - factor[v] * at
            row = jnp.broadcast_to(s[v0][k : k + 1, :], (8, B))
            for v in live:
                s[v] = s[v] - factor[v] * row
    out = []
    for v in range(tiles):
        root = lax.rsqrt(scale[v])
        root = root * (1.5 - 0.5 * scale[v] * root * root)
        out.append(jnp.where(lane <= sub + 8 * v, s[v] * root, 0.0))
    return out


def request_kernel(coarse_coords, coarse, coords, values, out_ref, place_ref, tile_ref):
    reps = values.shape[0]
    tile_ref[:reps, :] = values[...]
    tile_ref[reps:, :] = jnp.concatenate([coords[...], jnp.zeros((4, B), F32)], axis=0)
    tile, slot = coarse[...] // CP, coarse[...] % CP
    hot = (iota((B, COARSE), 0) == tile).astype(BF16)
    earlier = (iota((COARSE, COARSE), 0) < iota((COARSE, COARSE), 1)).astype(BF16)
    rank = jnp.sum(hot.astype(F32) * nn(hot, earlier, None), axis=0, keepdims=True).astype(jnp.int32)
    place_ref[...] = tile * MOST + rank
    asked = jnp.where(iota((B, COARSE), 0) == rank + 4 * CP, slot, 0).astype(F32).astype(BF16)
    line = jnp.concatenate([coarse_coords[k : k + 1, :] for k in range(4)] + [jnp.zeros((1, B - 4 * CP), F32)], axis=1)
    out_ref[...] = line + nt(hot, asked, None)


def send_kernel(table, coarse_values, after, send_ref):
    del after
    three = jnp.concatenate(thirds(coarse_values[...]), axis=0)
    slots = (iota((B, 3 * CP), 1) % CP).astype(F32)
    chunks = coarse_values.shape[1] // B
    for r in range(MOST):
        hot = (table[:, 4 * CP + r : 4 * CP + r + 1] == slots).astype(BF16)
        rows = nn(hot, three, None)
        for c in range(chunks):
            send_ref[pl.ds(r * chunks + c, B, stride=MOST * chunks), :] = rows[:, c * B : (c + 1) * B]


def spreads(theta, k, count):
    return jnp.exp(jnp.full((1, count), theta[1 + k], F32)) * RANGE_BASE


def pair(down, across, theta, live_down, live_across):
    squares = []
    for k in range(4):
        gap = down[:, k : k + 1] - across[k]
        squares.append(gap * gap)
    root = ROOT_FIVE * jnp.sqrt((squares[0] + squares[1]) + (squares[2] + squares[3]))
    variance = jnp.exp(jnp.full((1, live_across.shape[1]), theta[0], F32))
    paired = (live_down * live_across) * (variance * jnp.exp(-root))
    return paired * (1.0 + root + root * root * (1.0 / 3.0)), paired * ((5.0 / 3.0) * (1.0 + root)), squares


def nugget_of(theta, count):
    return NUGGET * jnp.exp(jnp.full((1, count), theta[5], F32))


def fine_kernel(theta, up, left, own, fine, d_ref, line_ref):
    up_hot = (iota((B, HALF), 0) == fine[:, :HALF]).astype(BF16)
    left_hot = (iota((B, HALF), 0) == fine[:, HALF:]).astype(BF16)
    upper_live = (lax.axis_index("row") > 0).astype(F32)
    picks = jnp.concatenate([picked(up[-8:, :], up_hot, nn) * upper_live, picked(left[-8:, :], left_hot, nn)], axis=1)
    across = [picks[k : k + 1] / spreads(theta, k, B) for k in range(4)]
    live = jnp.where(iota((1, B), 1) < HALF, upper_live, 1.0)
    lines = jnp.concatenate(across + [live, jnp.zeros((3, B), F32)], axis=0)
    line_ref[:, :B] = lines
    own_lines = [own[k : k + 1, :] / spreads(theta, k, B) for k in range(4)]
    line_ref[:, B:] = jnp.concatenate(own_lines + [jnp.ones((1, B), F32), jnp.zeros((3, B), F32)], axis=0)
    down = jnp.concatenate([lines, jnp.zeros((B - 8, B), F32)], axis=0).T
    kernel, _, _ = pair(down, across, theta, down[:, 4:5], live)
    same = iota((B, B), 0) == iota((B, B), 1)
    cov = kernel + jnp.where(same, live * nugget_of(theta, B) + 1.0 - live, 0.0)
    tiles = inverse_factor([cov[8 * v : 8 * (v + 1)] for v in range(B // 8)])
    for v in range(B // 8):
        d_ref[8 * v : 8 * (v + 1), :] = tiles[v]


def first_kernel(theta, table, lines, d_fine, coarse, m_ref, z_ref, g_ref, part_ref, k_ref, s_ref, d_ref, u_ref, left_ref, right_ref, f1_ref, f2_ref, f3_ref, y_ref):
    tile_hot = (iota((B, COARSE), 0) == coarse[...] // CP).astype(BF16)
    rows = picked(table[:, : 4 * CP], tile_hot, tn)
    wanted = (iota((4 * CP, COARSE), 0) % CP) == coarse[...] % CP
    rows = jnp.where(wanted, rows, 0.0)
    across = []
    for k in range(4):
        line = jnp.sum(rows[k * CP : (k + 1) * CP], axis=0, keepdims=True) / spreads(theta, k, COARSE)
        across.append(jnp.concatenate([lines[k : k + 1, :B], line, lines[k : k + 1, B:]], axis=1))
    live = jnp.concatenate([lines[4:5, :B], jnp.ones((1, N - B), F32)], axis=1)
    down = jnp.concatenate(across + [live] + [jnp.zeros((B - 5, N), F32)], axis=0).T
    nugget = nugget_of(theta, N)
    for r in range(N // B):
        here = slice(r * B, (r + 1) * B)
        kernel, common, squares = pair(down[here], across, theta, down[here, 4:5], live)
        for i, part in enumerate([kernel] + [common * square for square in squares]):
            f1_ref[i, here, :], f2_ref[i, here, :], f3_ref[i, here, :] = thirds(part)
        same = iota((B, N), 0) + r * B == iota((B, N), 1)
        k_ref[here, :] = kernel + jnp.where(same, live * nugget + 1.0 - live, 0.0)

    def prepare(p, d):
        at = pl.multiple_of(p * B, B)
        after = pl.multiple_of(p * B + B, B)
        u_ref[...] = nn(six_left(d), six_right(k_ref[pl.ds(at, B), :]), None)
        u_ref[:, pl.ds(at, B)] = -d
        k_ref[pl.ds(at, B), :] = jnp.zeros((B, N), F32)
        k_ref[:, pl.ds(at, B)] = jnp.zeros((N, B), F32)
        left_ref[...] = six_left(u_ref[...].T)
        right_ref[...] = six_right(u_ref[...])
        s_ref[...] = k_ref[pl.ds(after, B), pl.ds(after, B)] - nn(
            left_ref[pl.ds(after, B), :], right_ref[:, pl.ds(after, B)], None
        )

    prepare(0, d_fine[...])

    def sweep(p, carry):
        tiles = inverse_factor([s_ref[8 * v : 8 * (v + 1), :] for v in range(B // 8)])
        k_ref[...] -= nn(left_ref[...], right_ref[...], None)
        for v in range(B // 8):
            d_ref[8 * v : 8 * (v + 1), :] = tiles[v]

        @pl.when(p < N // B - 1)
        def _():
            prepare(p, d_ref[...])

        return carry

    lax.fori_loop(1, N // B, sweep, 0)
    d = d_ref[...]
    m_ref[:, :LEAD] = -nt(d, k_ref[:LEAD, LEAD:])
    m_ref[:, LEAD:] = d
    m = m_ref[...]
    parts = thirds(m)
    for i in range(5):
        first = nn(jnp.concatenate(parts, axis=0), f1_ref[i], None)
        second = nn(jnp.concatenate(parts[:2], axis=0), f2_ref[i], None)
        small = (first[2 * B :] + second[B:]) + nn(parts[0], f3_ref[i], None)
        y_ref[i * B : (i + 1) * B, :] = first[:B] + ((first[B : 2 * B] + second[:B]) + small)
    y_ref[5 * B :, :] = m * (live * nugget)
    high, low = halves(y_ref[...])
    z_ref[...] = -three_terms((high[:, :LEAD], low[:, :LEAD]), halves(k_ref[:LEAD, :LEAD]), nn)
    g_ref[...] = three_terms((high, low), parts[:2], nt)

    def folded(x):
        x = jnp.sum(x.reshape(B // 8, 8, x.shape[1]), axis=0)
        total = x[:, :B]
        for c in range(1, x.shape[1] // B):
            total = total + x[:, c * B : (c + 1) * B]
        return total

    sums = []
    for i in range(6):
        for j in range(i + 1):
            lead_part = z_ref[i * B : (i + 1) * B, :] * y_ref[j * B : (j + 1) * B, :LEAD]
            own_part = g_ref[i * B : (i + 1) * B, :] * g_ref[j * B : (j + 1) * B, :]
            sums.append(jnp.sum(2.0 * folded(lead_part) + folded(own_part), axis=0, keepdims=True))
    for i in range(6):
        sums.append(jnp.sum(folded(y_ref[i * B : (i + 1) * B, :] * m), axis=0, keepdims=True))
    sums.append(jnp.zeros((5, B), F32))
    part_ref[...] = jnp.concatenate(sums, axis=0)


def picked2(one_hot, table):
    high, low = halves(table)
    return nt(one_hot, high, None) + nt(one_hot, low, None)


def second_kernel(arrived, place, up, left, own, fine, m, z, g, part, white_ref, row_ref, v_ref):
    reps = own.shape[0]
    chunks = reps // B
    held = arrived.shape[0] // chunks
    down = jnp.concatenate([fine[...], place[...], jnp.zeros((1, B), jnp.int32)], axis=1)
    down = jnp.broadcast_to(down.astype(F32), (B, N)).T.astype(jnp.int32)[:, :1]
    hot = (down[:B] == iota((B, B), 1)).astype(BF16)
    v_ref[:HALF, :] = picked2(hot[:HALF], up[:reps, :])
    v_ref[HALF:B, :] = picked2(hot[HALF:], left[:reps, :])
    v_ref[LEAD:, :] = own[...].T
    hot = (down[B:LEAD] == iota((COARSE, held), 1)).astype(BF16)
    for c in range(chunks):
        high, low = halves(arrived[pl.ds(c, held, stride=chunks), :])
        v_ref[B:LEAD, c * B : (c + 1) * B] = nn(hot, high, None) + nn(hot, low, None)
    white = nn(m[...], v_ref[...])
    white_ref[...] = white.T
    cross = nt(white, v_ref[:LEAD, :])
    square = nt(white, white)
    lines = []
    for i in range(6):
        both = z[i * B : (i + 1) * B, :] * cross
        both = (both[:, :B] + both[:, B : 2 * B]) + (both[:, 2 * B : 3 * B] + both[:, 3 * B :])
        both = both + 0.5 * (g[i * B : (i + 1) * B, :] * square)
        lines.append(jnp.sum(both, axis=0, keepdims=True) - (0.5 * reps) * part[21 + i : 22 + i, :])
    whole = jnp.concatenate([(0.5 * reps) * part[:21, :]] + lines + [jnp.zeros((B - 27, B), F32)], axis=0)
    row_ref[...] = jnp.broadcast_to(jnp.sum(whole.T, axis=0, keepdims=True), row_ref.shape)


def third_kernel(rows, step_ref):
    total = jnp.broadcast_to(jnp.sum(rows[...], axis=0, keepdims=True), (8, B))
    sub, lane = iota((8, B), 0), iota((8, B), 1)
    a = jnp.zeros((8, B), F32)
    for i in range(6):
        for j in range(6):
            low, high = min(i, j), max(i, j)
            entry = jnp.broadcast_to(total[:, high * (high + 1) // 2 + low : high * (high + 1) // 2 + low + 1], (8, B))
            a = jnp.where((sub == i) & (lane == j), entry, a)
        entry = jnp.broadcast_to(total[:, 21 + i : 22 + i], (8, B))
        a = jnp.where((sub == i) & (lane == 6), entry, a)
    for k in range(6):
        row = jnp.broadcast_to(a[k : k + 1, :], (8, B))
        col = jnp.broadcast_to(a[:, k : k + 1], (8, B))
        row = row / jnp.broadcast_to(row[:, k : k + 1], (8, B))
        a = jnp.where(sub == k, row, a - col * row)
    step_ref[...] = jnp.sum(jnp.where((lane == sub) & (sub < 6), jnp.broadcast_to(a[:, 6:7], (8, B)), 0.0), axis=0)[:6]


def body(coords, values, coarse_coords, coarse_values, fine_index, coarse_index, log_params):
    reps = values.shape[0]
    devices = lax.axis_size("row") * lax.axis_size("col")
    vmem = pl.BlockSpec(memory_space=pltpu.VMEM)
    smem = pl.BlockSpec(memory_space=pltpu.SMEM)
    large = pltpu.CompilerParams(vmem_limit_bytes=60 * 2**20)

    def shape(*dims):
        return jax.ShapeDtypeStruct(dims, F32)

    def cost(flops):
        return pl.CostEstimate(flops=flops, bytes_accessed=2**20, transcendentals=0)

    request, place, tile = pl.pallas_call(
        request_kernel,
        out_shape=(shape(devices, B), jax.ShapeDtypeStruct((1, COARSE), jnp.int32), shape(reps + 8, B)),
        in_specs=[vmem] * 4,
        out_specs=(vmem,) * 3,
        compiler_params=large,
        name="request_part",
    )(coarse_coords, coarse_index, coords, values)
    up = shifted(tile, "row", 1)
    left = passed_along(tile, "col", 1)
    table = lax.all_to_all(request, AXES, 0, 0, tiled=True)
    d_fine, lines = pl.pallas_call(
        fine_kernel,
        out_shape=(shape(B, B), shape(8, 2 * B)),
        in_specs=[smem] + [vmem] * 4,
        out_specs=(vmem,) * 2,
        compiler_params=large,
        cost_estimate=cost(4 * 10**9),
        name="fine_part",
    )(log_params, up, left, coords, fine_index)
    send = pl.pallas_call(
        send_kernel,
        out_shape=shape(devices * MOST * reps // B, B),
        in_specs=[vmem] * 2 + [pl.BlockSpec(memory_space=pl.ANY)],
        out_specs=vmem,
        compiler_params=large,
        name="send_part",
    )(table, coarse_values.T, lines)
    arrived = lax.all_to_all(send, AXES, 0, 0, tiled=True)
    m, z, g, part = pl.pallas_call(
        first_kernel,
        out_shape=(shape(B, N), shape(6 * B, LEAD), shape(6 * B, B), shape(32, B)),
        in_specs=[smem] + [vmem] * 4,
        out_specs=(vmem,) * 4,
        scratch_shapes=[
            pltpu.VMEM((N, N), F32),
            pltpu.VMEM((B, B), F32),
            pltpu.VMEM((B, B), F32),
            pltpu.VMEM((B, N), F32),
            pltpu.VMEM((N, 6 * B), BF16),
            pltpu.VMEM((6 * B, N), BF16),
            pltpu.VMEM((5, N, N), BF16),
            pltpu.VMEM((5, N, N), BF16),
            pltpu.VMEM((5, N, N), BF16),
            pltpu.VMEM((6 * B, N), F32),
        ],
        compiler_params=large,
        cost_estimate=cost(30 * 10**9),
        name="fisher_part",
    )(log_params, table, lines, d_fine, coarse_index)
    white, row = pl.pallas_call(
        second_kernel,
        out_shape=(shape(reps, B), shape(devices, B)),
        in_specs=[vmem] * 10,
        out_specs=(vmem,) * 2,
        scratch_shapes=[pltpu.VMEM((N, reps), F32)],
        compiler_params=large,
        name="gradient_part",
    )(arrived, place, up, left, values, fine_index, m, z, g, part)
    rows = lax.all_to_all(row, AXES, 0, 0, tiled=True)
    step = pl.pallas_call(
        third_kernel,
        out_shape=shape(6),
        in_specs=[vmem],
        out_specs=vmem,
        compiler_params=large,
        name="solve_part",
    )(rows)
    return (step, white)


def solution(mesh):
    in_specs = (
        P(None, AXES),
        P(None, AXES),
        P(None, AXES),
        P(None, AXES),
        P(AXES, None),
        P(AXES, None),
        P(),
    )
    out_specs = (P(), P(None, AXES))
    return jax.shard_map(body, mesh=mesh, in_specs=in_specs, out_specs=out_specs, check_vma=False)
```

```python
import math

import jax
import jax.numpy as jnp
from jax import lax
from jax.experimental import pallas as pl
from jax.experimental.pallas import tpu as pltpu
from jax.sharding import PartitionSpec as P

HIGH = lax.Precision.HIGHEST
ROOT_FIVE = math.sqrt(5.0)
NUGGET = 0.2
RANGE_BASE = 0.5
F32 = jnp.float32
BF16 = jnp.bfloat16
AXES = ("row", "col")

B = 128
N = 640
LEAD = 512
COARSE = 384
HALF = 64
CP = 16
MOST = 6
FINE, PLACE, WANTED, SPREAD, VARIANCE, NUG, TAIL = 4, 5, 8, 11, 15, 16, 24
MROW, PROW, FIELDS = 768, 896, 928


def shifted(value, axis, steps):
    count = lax.axis_size(axis)
    first, last = (max(0, -steps), min(count, count - steps))
    return lax.ppermute(value, axis, [(source, source + steps) for source in range(first, last)])


def passed_along(block, axis, distance):
    devices = range(lax.axis_size(axis))
    route = [((i - distance) % len(devices), i) for i in devices]
    return lax.ppermute(block, axis, route)


def nn(a, b, precision=HIGH):
    return lax.dot_general(a, b, (((1,), (0,)), ((), ())), precision=precision, preferred_element_type=F32)


def nt(a, b, precision=HIGH):
    return lax.dot_general(a, b, (((1,), (1,)), ((), ())), precision=precision, preferred_element_type=F32)


def tn(a, b, precision=HIGH):
    return lax.dot_general(a, b, (((0,), (0,)), ((), ())), precision=precision, preferred_element_type=F32)


def iota(shape, dim):
    return lax.broadcasted_iota(jnp.int32, shape, dim)


def halves(x):
    high = x.astype(BF16)
    return high, (x - high.astype(F32)).astype(BF16)


def thirds(x):
    high = x.astype(BF16)
    rest = x - high.astype(F32)
    mid = rest.astype(BF16)
    return high, mid, (rest - mid.astype(F32)).astype(BF16)


def picked(table, one_hot, dot):
    high, mid, low = thirds(table)
    return (dot(high, one_hot, None) + dot(mid, one_hot, None)) + dot(low, one_hot, None)


def six_left(x):
    one, two, three = thirds(x)
    return jnp.concatenate([one, one, two, two, one, three], axis=1)


def six_right(x):
    one, two, three = thirds(x)
    return jnp.concatenate([one, two, one, two, three, one], axis=0)


def three_terms(left, right, dot):
    rows = left[0].shape[0]
    both = dot(jnp.concatenate(left, axis=0), right[0], None)
    return (both[:rows] + both[rows:]) + dot(left[0], right[1], None)


def wide(x, j):
    return jnp.broadcast_to(x[:, j : j + 1], (8, B))


def tall(x, k):
    return jnp.broadcast_to(x[k : k + 1, :], (8, B))


def inverse_factor(s):
    tiles = B // 8
    s = list(s)
    sub, lane = iota((8, B), 0), iota((8, B), 1)
    out = []
    ahead = [wide(s[0], j) for j in range(8)]
    for g in range(tiles):
        k0 = 8 * g
        live = range(g, tiles)
        cols = [{v: wide(s[v], k0 + j) for v in range(g + 1, tiles)} for j in range(8)]
        for j in range(8):
            cols[j][g] = ahead[j]
        if g + 1 < tiles:
            ahead = [wide(s[g + 1], k0 + 8 + j) for j in range(8)]
        inside = (lane >= k0) & (lane < k0 + 8)
        s[g] = jnp.where(inside, (lane == sub + k0).astype(F32), s[g])
        for v in range(g + 1, tiles):
            s[v] = jnp.where(inside, 0.0, s[v])
        pivots = jnp.ones((8, B), F32)
        pivot = tall(cols[0][g], 0)
        for k in range(8):
            col = cols[k]
            pivots = jnp.where(sub == k, pivot, pivots)
            over = 1.0 / pivot
            if k < 7:
                below = tall(col[g], k + 1)
                pivot = tall(cols[k + 1][g], k + 1) - (below * below) * over
            factor = {v: col[v] * over for v in live}
            factor[g] = jnp.where(sub > k, factor[g], 0.0)
            for later in range(k + 1, 8):
                at = tall(col[g], later)
                for v in live:
                    cols[later][v] = cols[later][v] - factor[v] * at
            if g + 1 < tiles:
                for j in range(8):
                    ahead[j] = ahead[j] - factor[g + 1] * tall(col[g + 1], j)
            row = tall(s[g], k)
            for v in live:
                s[v] = s[v] - factor[v] * row
        root = lax.rsqrt(pivots)
        root = root * (1.5 - 0.5 * pivots * root * root)
        out.append(jnp.where(lane <= sub + k0, s[g] * root, 0.0))
    return out


def request_kernel(theta, coarse_coords, coarse, coords, values, fine, out_ref, tile_ref):
    reps = values.shape[0]
    tile, slot = coarse[...] // CP, coarse[...] % CP
    hot = (iota((B, COARSE), 0) == tile).astype(BF16)
    earlier = (iota((COARSE, COARSE), 0) < iota((COARSE, COARSE), 1)).astype(BF16)
    rank = jnp.sum(hot.astype(F32) * nn(hot, earlier, None), axis=0, keepdims=True).astype(jnp.int32)
    asked = jnp.where(iota((B, COARSE), 0) == rank + 4 * CP, slot, 0).astype(F32).astype(BF16)
    line = jnp.concatenate([coarse_coords[k : k + 1, :] for k in range(4)] + [jnp.zeros((1, B - 4 * CP), F32)], axis=1)
    out_ref[...] = line + nt(hot, asked, None)
    place = (tile * MOST + rank).astype(F32)
    wanted = coarse[...].astype(F32)
    rows = [coords[...], fine[...].astype(F32)]
    rows += [place[:, c * B : (c + 1) * B] for c in range(COARSE // B)]
    rows += [wanted[:, c * B : (c + 1) * B] for c in range(COARSE // B)]
    rows += [jnp.exp(jnp.full((1, B), theta[1 + k], F32)) * RANGE_BASE for k in range(4)]
    rows += [jnp.exp(jnp.full((1, B), theta[0], F32)), NUGGET * jnp.exp(jnp.full((1, B), theta[5], F32))]
    rows += [jnp.zeros((TAIL - NUG - 1, B), F32)]
    tile_ref[:reps, :] = values[...]
    tile_ref[reps:, :] = jnp.concatenate(rows, axis=0)


def send_kernel(table, coarse_values, after, send_ref):
    del after
    three = jnp.concatenate(thirds(coarse_values[...]), axis=0)
    slots = (iota((B, 3 * CP), 1) % CP).astype(F32)
    chunks = coarse_values.shape[1] // B
    for r in range(MOST):
        hot = (table[:, 4 * CP + r : 4 * CP + r + 1] == slots).astype(BF16)
        rows = nn(hot, three, None)
        for c in range(chunks):
            send_ref[pl.ds(r * chunks + c, B, stride=MOST * chunks), :] = rows[:, c * B : (c + 1) * B]


def pair(down, across, variance, live_down, live_across):
    squares = []
    for k in range(4):
        gap = down[:, k : k + 1] - across[k]
        squares.append(gap * gap)
    root = ROOT_FIVE * jnp.sqrt((squares[0] + squares[1]) + (squares[2] + squares[3]))
    paired = (live_down * live_across) * (variance * jnp.exp(-root))
    return paired * (1.0 + root + root * root * (1.0 / 3.0)), paired * ((5.0 / 3.0) * (1.0 + root)), squares


def fine_kernel(tile, up, left, out_ref):
    reps = tile.shape[0] - TAIL
    tail = tile[reps:, :]
    fine = tail[FINE : FINE + 1, :]
    column = iota((B, HALF), 0).astype(F32)
    up_hot = (column == fine[:, :HALF]).astype(BF16)
    left_hot = (column == fine[:, HALF:]).astype(BF16)
    upper_live = (lax.axis_index("row") > 0).astype(F32)
    picks = jnp.concatenate(
        [picked(up[reps : reps + 8, :], up_hot, nn) * upper_live, picked(left[reps : reps + 8, :], left_hot, nn)], axis=1
    )
    across = [picks[k : k + 1] / tail[SPREAD + k : SPREAD + k + 1] for k in range(4)]
    live = jnp.where(iota((1, B), 1) < HALF, upper_live, 1.0)
    lines = jnp.concatenate(across + [live, jnp.zeros((3, B), F32)], axis=0)
    own_lines = [tail[k : k + 1, :] / tail[SPREAD + k : SPREAD + k + 1] for k in range(4)]
    own_lines = jnp.concatenate(own_lines + [jnp.ones((1, B), F32), jnp.zeros((3, B), F32)], axis=0)
    thrice = jnp.concatenate([tail[SPREAD : NUG + 1, :]] * 3, axis=1)
    ends = [jnp.concatenate([tail[n + c : n + c + 1, :] for c in range(3)], axis=1) for n in (PLACE, WANTED)]
    out_ref[2 * B :, :] = jnp.concatenate([lines, own_lines, jnp.concatenate(ends + [thrice], axis=0)], axis=1)
    down = jnp.concatenate([lines, jnp.zeros((B - 8, B), F32)], axis=0).T
    kernel, _, _ = pair(down, across, tail[VARIANCE : VARIANCE + 1, :], down[:, 4:5], live)
    same = iota((B, B), 0) == iota((B, B), 1)
    cov = kernel + jnp.where(same, live * tail[NUG : NUG + 1, :] + 1.0 - live, 0.0)
    tiles = inverse_factor([cov[8 * v : 8 * (v + 1)] for v in range(B // 8)])
    for v in range(B // 8):
        out_ref[8 * v : 8 * (v + 1), reps:] = tiles[v]
    hot = (jnp.broadcast_to(fine, (B, B)).T == iota((B, B), 1).astype(F32)).astype(BF16)
    out_ref[:HALF, :reps] = picked2(hot[:HALF], up[:reps, :])
    out_ref[HALF:B, :reps] = picked2(hot[HALF:], left[:reps, :])
    out_ref[B : 2 * B, :reps] = tile[:reps, :].T
    out_ref[B : 2 * B, reps:] = jnp.zeros((B, B), F32)


def first_kernel(table, given, out_ref, k_ref, s_ref, d_ref, u_ref, left_ref, right_ref, f_ref, f3_ref, y_ref):
    lines = given[2 * B :, : 2 * B]
    ends = given[2 * B :, 2 * B :]
    wanted = ends[1:2].astype(jnp.int32)
    tile_hot = (iota((B, COARSE), 0) == wanted // CP).astype(BF16)
    rows = picked(table[:, : 4 * CP], tile_hot, tn)
    rows = jnp.where((iota((4 * CP, COARSE), 0) % CP) == wanted % CP, rows, 0.0)
    across = []
    for k in range(4):
        line = jnp.sum(rows[k * CP : (k + 1) * CP], axis=0, keepdims=True) / ends[2 + k : 3 + k]
        across.append(jnp.concatenate([lines[k : k + 1, :B], line, lines[k : k + 1, B:]], axis=1))
    live = jnp.concatenate([lines[4:5, :B], jnp.ones((1, N - B), F32)], axis=1)
    down = jnp.concatenate(across + [live] + [jnp.zeros((B - 5, N), F32)], axis=0).T
    variance = jnp.concatenate([ends[6:7], ends[6:7, : N - COARSE]], axis=1)
    nugget = jnp.concatenate([ends[7:8], ends[7:8, : N - COARSE]], axis=1)
    out_ref[FIELDS : FIELDS + 2 * B, :LEAD] = given[: 2 * B, :LEAD]
    out_ref[FIELDS:, LEAD:] = jnp.broadcast_to(ends[0:1], (B, COARSE)).T
    for r in range(N // B):
        here = slice(r * B, (r + 1) * B)
        kernel, common, squares = pair(down[here], across, variance, down[here, 4:5], live)
        for i, part in enumerate([kernel] + [common * square for square in squares]):
            there = slice(i * N, (i + 1) * N)
            f_ref[here, there], f_ref[N + r * B : N + (r + 1) * B, there], f3_ref[here, there] = thirds(part)
        same = iota((B, N), 0) + r * B == iota((B, N), 1)
        k_ref[here, :] = kernel + jnp.where(same, live * nugget + 1.0 - live, 0.0)

    def conditional(p):
        at = pl.multiple_of(p * B, B)
        after = pl.multiple_of(p * B + B, B)
        u = nn(six_left(d_ref[...]), six_right(k_ref[pl.ds(at, B), pl.ds(after, B)]), None)
        s_ref[...] = k_ref[pl.ds(after, B), pl.ds(after, B)] - nn(six_left(u.T), six_right(u), None)

    d_ref[...] = given[:B, LEAD:]
    conditional(0)

    def sweep(p, carry):
        tiles = inverse_factor([s_ref[8 * v : 8 * (v + 1), :] for v in range(B // 8)])
        last = pl.multiple_of(p * B - B, B)
        d = d_ref[...]
        u_ref[...] = nn(six_left(d), six_right(k_ref[pl.ds(last, B), :]), None)
        u_ref[:, pl.ds(last, B)] = -d
        k_ref[pl.ds(last, B), :] = jnp.zeros((B, N), F32)
        k_ref[:, pl.ds(last, B)] = jnp.zeros((N, B), F32)
        left_ref[...] = six_left(u_ref[...].T)
        right_ref[...] = six_right(u_ref[...])
        k_ref[...] -= nn(left_ref[...], right_ref[...], None)
        for v in range(B // 8):
            d_ref[8 * v : 8 * (v + 1), :] = tiles[v]

        @pl.when(p < N // B - 1)
        def _():
            conditional(p)

        return carry

    lax.fori_loop(1, N // B, sweep, 0)
    d = d_ref[...]
    out_ref[MROW : MROW + B, :LEAD] = -nt(d, k_ref[:LEAD, LEAD:])
    out_ref[MROW : MROW + B, LEAD:] = d
    m = out_ref[MROW : MROW + B, :]
    parts = halves(m)
    twice = jnp.concatenate([jnp.concatenate([part, part], axis=1) for part in parts], axis=0)
    large = nn(twice, f_ref[...], None)
    small = large[B:] + nn(parts[0], f3_ref[...], None)
    for i in range(5):
        there = slice(i * N, (i + 1) * N)
        y_ref[i * B : (i + 1) * B, :] = large[:B, there] + small[:, there]
    y_ref[5 * B :, :] = m * (live * nugget)
    high, low = halves(y_ref[...])
    out_ref[:MROW, :LEAD] = -three_terms((high[:, :LEAD], low[:, :LEAD]), halves(k_ref[:LEAD, :LEAD]), nn)
    out_ref[:MROW, LEAD:] = three_terms((high, low), parts, nt)

    def folded(x):
        x = jnp.sum(x.reshape(B // 8, 8, x.shape[1]), axis=0)
        total = x[:, :B]
        for c in range(1, x.shape[1] // B):
            total = total + x[:, c * B : (c + 1) * B]
        return total

    sums = []
    for i in range(6):
        for j in range(i + 1):
            lead_part = out_ref[i * B : (i + 1) * B, :LEAD] * y_ref[j * B : (j + 1) * B, :LEAD]
            own_part = out_ref[i * B : (i + 1) * B, LEAD:] * out_ref[j * B : (j + 1) * B, LEAD:]
            sums.append(jnp.sum(2.0 * folded(lead_part) + folded(own_part), axis=0, keepdims=True))
    for i in range(6):
        sums.append(jnp.sum(folded(y_ref[i * B : (i + 1) * B, :] * m), axis=0, keepdims=True))
    sums.append(jnp.zeros((5, B), F32))
    out_ref[PROW:FIELDS, :B] = jnp.concatenate(sums, axis=0)


def picked2(one_hot, table):
    high, low = halves(table)
    return nt(one_hot, high, None) + nt(one_hot, low, None)


def second_kernel(arrived, parts, white_ref, row_ref, v_ref, given, sems):
    pieces = ((FIELDS, FIELDS + COARSE), (MROW, FIELDS), (0, MROW))
    copies = [
        pltpu.make_async_copy(parts.at[first:end], given.at[first:end], sems.at[n]) for n, (first, end) in enumerate(pieces)
    ]
    for copy in copies:
        copy.start()
    copies[0].wait()
    reps = white_ref.shape[0]
    chunks = reps // B
    held = arrived.shape[0] // chunks
    v_ref[:B, :] = given[FIELDS : FIELDS + B, :reps]
    v_ref[LEAD:, :] = given[FIELDS + B : FIELDS + 2 * B, :reps]
    hot = (given[FIELDS:, LEAD : LEAD + 1] == iota((COARSE, held), 1).astype(F32)).astype(BF16)
    for c in range(chunks):
        high, low = halves(arrived[pl.ds(c, held, stride=chunks), :])
        v_ref[B:LEAD, c * B : (c + 1) * B] = nn(hot, high, None) + nn(hot, low, None)
    copies[1].wait()
    white = nn(given[MROW : MROW + B, :], v_ref[...])
    white_ref[...] = white.T
    cross = nt(white, v_ref[:LEAD, :])
    square = nt(white, white)
    copies[2].wait()
    part = given[PROW:FIELDS, :B]
    lines = []
    for i in range(6):
        both = given[i * B : (i + 1) * B, :LEAD] * cross
        both = (both[:, :B] + both[:, B : 2 * B]) + (both[:, 2 * B : 3 * B] + both[:, 3 * B :])
        both = both + 0.5 * (given[i * B : (i + 1) * B, LEAD:] * square)
        lines.append(jnp.sum(both, axis=0, keepdims=True) - (0.5 * reps) * part[21 + i : 22 + i, :])
    whole = jnp.concatenate([(0.5 * reps) * part[:21, :]] + lines + [jnp.zeros((B - 27, B), F32)], axis=0)
    row_ref[...] = jnp.broadcast_to(jnp.sum(whole.T, axis=0, keepdims=True), row_ref.shape)


def third_kernel(rows, step_ref):
    total = jnp.broadcast_to(jnp.sum(rows[...], axis=0, keepdims=True), (8, B))
    sub, lane = iota((8, B), 0), iota((8, B), 1)
    a = jnp.zeros((8, B), F32)
    for i in range(6):
        for j in range(6):
            low, high = min(i, j), max(i, j)
            entry = jnp.broadcast_to(total[:, high * (high + 1) // 2 + low : high * (high + 1) // 2 + low + 1], (8, B))
            a = jnp.where((sub == i) & (lane == j), entry, a)
        entry = jnp.broadcast_to(total[:, 21 + i : 22 + i], (8, B))
        a = jnp.where((sub == i) & (lane == 6), entry, a)
    for k in range(6):
        row = jnp.broadcast_to(a[k : k + 1, :], (8, B))
        col = jnp.broadcast_to(a[:, k : k + 1], (8, B))
        row = row / jnp.broadcast_to(row[:, k : k + 1], (8, B))
        a = jnp.where(sub == k, row, a - col * row)
    step_ref[...] = jnp.sum(jnp.where((lane == sub) & (sub < 6), jnp.broadcast_to(a[:, 6:7], (8, B)), 0.0), axis=0)[:6]


def body(coords, values, coarse_coords, coarse_values, fine_index, coarse_index, log_params):
    reps = values.shape[0]
    devices = lax.axis_size("row") * lax.axis_size("col")
    vmem = pl.BlockSpec(memory_space=pltpu.VMEM)
    smem = pl.BlockSpec(memory_space=pltpu.SMEM)

    def shape(*dims):
        return jax.ShapeDtypeStruct(dims, F32)

    def cost(flops):
        return pl.CostEstimate(flops=flops, bytes_accessed=2**20, transcendentals=0)

    def room(mib):
        return pltpu.CompilerParams(vmem_limit_bytes=mib * 2**20)

    request, tile = pl.pallas_call(
        request_kernel,
        out_shape=(shape(devices, B), shape(reps + TAIL, B)),
        in_specs=[smem] + [vmem] * 5,
        out_specs=(vmem,) * 2,
        compiler_params=room(60),
        name="request_part",
    )(log_params, coarse_coords, coarse_index, coords, values, fine_index)
    up = shifted(tile, "row", 1)
    left = passed_along(tile, "col", 1)
    table = lax.all_to_all(request, AXES, 0, 0, tiled=True)
    fine = pl.pallas_call(
        fine_kernel,
        out_shape=shape(2 * B + 8, N),
        in_specs=[vmem] * 3,
        out_specs=vmem,
        compiler_params=room(8),
        cost_estimate=cost(4 * 10**9),
        name="fine_part",
    )(tile, up, left)
    send = pl.pallas_call(
        send_kernel,
        out_shape=shape(devices * MOST * reps // B, B),
        in_specs=[vmem] * 2 + [pl.BlockSpec(memory_space=pl.ANY)],
        out_specs=vmem,
        compiler_params=room(8),
        name="send_part",
    )(table, coarse_values.T, fine)
    arrived = lax.all_to_all(send, AXES, 0, 0, tiled=True)
    parts = pl.pallas_call(
        first_kernel,
        out_shape=shape(FIELDS + COARSE, N),
        in_specs=[vmem] * 2,
        out_specs=vmem,
        scratch_shapes=[
            pltpu.VMEM((N, N), F32),
            pltpu.VMEM((B, B), F32),
            pltpu.VMEM((B, B), F32),
            pltpu.VMEM((B, N), F32),
            pltpu.VMEM((N, 6 * B), BF16),
            pltpu.VMEM((6 * B, N), BF16),
            pltpu.VMEM((2 * N, 5 * N), BF16),
            pltpu.VMEM((N, 5 * N), BF16),
            pltpu.VMEM((6 * B, N), F32),
        ],
        compiler_params=room(36),
        cost_estimate=cost(30 * 10**9),
        name="fisher_part",
    )(table, fine)
    white, row = pl.pallas_call(
        second_kernel,
        out_shape=(shape(reps, B), shape(devices, B)),
        in_specs=[vmem, pl.BlockSpec(memory_space=pl.ANY)],
        out_specs=(vmem,) * 2,
        scratch_shapes=[
            pltpu.VMEM((N, reps), F32),
            pltpu.VMEM((FIELDS + COARSE, N), F32),
            pltpu.SemaphoreType.DMA((3,)),
        ],
        compiler_params=room(24),
        name="gradient_part",
    )(arrived, parts)
    rows = lax.all_to_all(row, AXES, 0, 0, tiled=True)
    step = pl.pallas_call(
        third_kernel,
        out_shape=shape(6),
        in_specs=[vmem],
        out_specs=vmem,
        compiler_params=room(8),
        name="solve_part",
    )(rows)
    return (step, white)


def solution(mesh):
    in_specs = (
        P(None, AXES),
        P(None, AXES),
        P(None, AXES),
        P(None, AXES),
        P(AXES, None),
        P(AXES, None),
        P(),
    )
    out_specs = (P(), P(None, AXES))
    return jax.shard_map(body, mesh=mesh, in_specs=in_specs, out_specs=out_specs, check_vma=False)
```

```python
import math

import jax
import jax.numpy as jnp
from jax import lax
from jax.experimental import pallas as pl
from jax.experimental.pallas import tpu as pltpu
from jax.sharding import PartitionSpec as P

HIGH = lax.Precision.HIGHEST
ROOT_FIVE = math.sqrt(5.0)
NUGGET = 0.2
RANGE_BASE = 0.5
F32 = jnp.float32
BF16 = jnp.bfloat16
AXES = ("row", "col")

B = 128
N = 640
LEAD = 512
COARSE = 384
HALF = 64
CP = 16
MOST = 6
FINE, PLACE, WANTED, SPREAD, VARIANCE, NUG, TAIL = 4, 5, 8, 11, 15, 16, 24
MROW, PROW, FIELDS = 768, 896, 928


def shifted(value, axis, steps):
    count = lax.axis_size(axis)
    first, last = (max(0, -steps), min(count, count - steps))
    return lax.ppermute(value, axis, [(source, source + steps) for source in range(first, last)])


def passed_along(block, axis, distance):
    devices = range(lax.axis_size(axis))
    route = [((i - distance) % len(devices), i) for i in devices]
    return lax.ppermute(block, axis, route)


def nn(a, b, precision=HIGH):
    return lax.dot_general(a, b, (((1,), (0,)), ((), ())), precision=precision, preferred_element_type=F32)


def nt(a, b, precision=HIGH):
    return lax.dot_general(a, b, (((1,), (1,)), ((), ())), precision=precision, preferred_element_type=F32)


def tn(a, b, precision=HIGH):
    return lax.dot_general(a, b, (((0,), (0,)), ((), ())), precision=precision, preferred_element_type=F32)


def iota(shape, dim):
    return lax.broadcasted_iota(jnp.int32, shape, dim)


def halves(x):
    high = x.astype(BF16)
    return high, (x - high.astype(F32)).astype(BF16)


def thirds(x):
    high = x.astype(BF16)
    rest = x - high.astype(F32)
    mid = rest.astype(BF16)
    return high, mid, (rest - mid.astype(F32)).astype(BF16)


def picked(table, one_hot, dot):
    high, mid, low = thirds(table)
    return (dot(high, one_hot, None) + dot(mid, one_hot, None)) + dot(low, one_hot, None)


def six_left(x):
    one, two, three = thirds(x)
    return jnp.concatenate([one, one, two, two, one, three], axis=1)


def six_right(x):
    one, two, three = thirds(x)
    return jnp.concatenate([one, two, one, two, three, one], axis=0)


def three_terms(left, right, dot):
    rows = left[0].shape[0]
    both = dot(jnp.concatenate(left, axis=0), right[0], None)
    return (both[:rows] + both[rows:]) + dot(left[0], right[1], None)


def wide(x, j):
    return jnp.broadcast_to(x[:, j : j + 1], (8, B))


def tall(x, k):
    return jnp.broadcast_to(x[k : k + 1, :], (8, B))


def inverse_factor(s):
    tiles = B // 8
    s = list(s)
    sub, lane = iota((8, B), 0), iota((8, B), 1)
    out = []
    ahead = [wide(s[0], j) for j in range(8)]
    for g in range(tiles):
        k0 = 8 * g
        more = g + 1 < tiles
        cols = ahead
        inside = (lane >= k0) & (lane < k0 + 8)
        mine = jnp.where(inside, (lane == sub + k0).astype(F32), s[g])
        if more:
            near = [wide(s[g + 1], k0 + j) for j in range(8)]
            ahead = [wide(s[g + 1], k0 + 8 + j) for j in range(8)]
            after = jnp.where(inside, 0.0, s[g + 1])
        pivots = jnp.ones((8, B), F32)
        pivot = tall(cols[0], 0)
        scaled, rows = [], []
        for k in range(8):
            pivots = jnp.where(sub == k, pivot, pivots)
            over = 1.0 / pivot
            at = [tall(cols[k], later) for later in range(k + 1, 8)]
            if k < 7:
                pivot = tall(cols[k + 1], k + 1) - (at[0] * at[0]) * over
            at = [entry * over for entry in at]
            row = tall(mine, k) * over
            column = jnp.where(sub > k, cols[k], 0.0)
            for later in range(k + 1, 8):
                cols[later] = cols[later] - column * at[later - k - 1]
            mine = mine - column * row
            scaled.append(at)
            rows.append(row)
            if more:
                for later in range(k + 1, 8):
                    near[later] = near[later] - near[k] * at[later - k - 1]
                for j in range(8):
                    ahead[j] = ahead[j] - near[k] * (tall(near[k], j) * over)
                after = after - near[k] * row
        if more:
            s[g + 1] = after
        for v in range(g + 2, tiles):
            col = [wide(s[v], k0 + j) for j in range(8)]
            x = jnp.where(inside, 0.0, s[v])
            for k in range(8):
                for later in range(k + 1, 8):
                    col[later] = col[later] - col[k] * scaled[k][later - k - 1]
                x = x - col[k] * rows[k]
            s[v] = x
        root = lax.rsqrt(pivots)
        root = root * (1.5 - 0.5 * pivots * root * root)
        out.append(jnp.where(lane <= sub + k0, mine * root, 0.0))
    return out


def request_kernel(theta, coarse_coords, coarse, coords, values, fine, out_ref, tile_ref):
    reps = values.shape[0]
    tile, slot = coarse[...] // CP, coarse[...] % CP
    hot = (iota((B, COARSE), 0) == tile).astype(BF16)
    earlier = (iota((COARSE, COARSE), 0) < iota((COARSE, COARSE), 1)).astype(BF16)
    rank = jnp.sum(hot.astype(F32) * nn(hot, earlier, None), axis=0, keepdims=True).astype(jnp.int32)
    asked = jnp.where(iota((B, COARSE), 0) == rank + 4 * CP, slot, 0).astype(F32).astype(BF16)
    line = jnp.concatenate([coarse_coords[k : k + 1, :] for k in range(4)] + [jnp.zeros((1, B - 4 * CP), F32)], axis=1)
    out_ref[...] = line + nt(hot, asked, None)
    place = (tile * MOST + rank).astype(F32)
    wanted = coarse[...].astype(F32)
    rows = [coords[...], fine[...].astype(F32)]
    rows += [place[:, c * B : (c + 1) * B] for c in range(COARSE // B)]
    rows += [wanted[:, c * B : (c + 1) * B] for c in range(COARSE // B)]
    rows += [jnp.exp(jnp.full((1, B), theta[1 + k], F32)) * RANGE_BASE for k in range(4)]
    rows += [jnp.exp(jnp.full((1, B), theta[0], F32)), NUGGET * jnp.exp(jnp.full((1, B), theta[5], F32))]
    rows += [jnp.zeros((TAIL - NUG - 1, B), F32)]
    tile_ref[:reps, :] = values[...]
    tile_ref[reps:, :] = jnp.concatenate(rows, axis=0)


def send_kernel(table, coarse_values, after, send_ref):
    del after
    three = jnp.concatenate(thirds(coarse_values[...]), axis=0)
    slots = (iota((B, 3 * CP), 1) % CP).astype(F32)
    chunks = coarse_values.shape[1] // B
    for r in range(MOST):
        hot = (table[:, 4 * CP + r : 4 * CP + r + 1] == slots).astype(BF16)
        rows = nn(hot, three, None)
        for c in range(chunks):
            send_ref[pl.ds(r * chunks + c, B, stride=MOST * chunks), :] = rows[:, c * B : (c + 1) * B]


def pair(down, across, variance, live_down, live_across):
    squares = []
    for k in range(4):
        gap = down[:, k : k + 1] - across[k]
        squares.append(gap * gap)
    root = ROOT_FIVE * jnp.sqrt((squares[0] + squares[1]) + (squares[2] + squares[3]))
    paired = (live_down * live_across) * (variance * jnp.exp(-root))
    return paired * (1.0 + root + root * root * (1.0 / 3.0)), paired * ((5.0 / 3.0) * (1.0 + root)), squares


def fine_kernel(tile, up, left, out_ref):
    reps = tile.shape[0] - TAIL
    tail = tile[reps:, :]
    fine = tail[FINE : FINE + 1, :]
    column = iota((B, HALF), 0).astype(F32)
    up_hot = (column == fine[:, :HALF]).astype(BF16)
    left_hot = (column == fine[:, HALF:]).astype(BF16)
    upper_live = (lax.axis_index("row") > 0).astype(F32)
    picks = jnp.concatenate(
        [picked(up[reps : reps + 8, :], up_hot, nn) * upper_live, picked(left[reps : reps + 8, :], left_hot, nn)], axis=1
    )
    across = [picks[k : k + 1] / tail[SPREAD + k : SPREAD + k + 1] for k in range(4)]
    live = jnp.where(iota((1, B), 1) < HALF, upper_live, 1.0)
    lines = jnp.concatenate(across + [live, jnp.zeros((3, B), F32)], axis=0)
    own_lines = [tail[k : k + 1, :] / tail[SPREAD + k : SPREAD + k + 1] for k in range(4)]
    own_lines = jnp.concatenate(own_lines + [jnp.ones((1, B), F32), jnp.zeros((3, B), F32)], axis=0)
    thrice = jnp.concatenate([tail[SPREAD : NUG + 1, :]] * 3, axis=1)
    ends = [jnp.concatenate([tail[n + c : n + c + 1, :] for c in range(3)], axis=1) for n in (PLACE, WANTED)]
    out_ref[2 * B :, :] = jnp.concatenate([lines, own_lines, jnp.concatenate(ends + [thrice], axis=0)], axis=1)
    down = jnp.concatenate([lines, jnp.zeros((B - 8, B), F32)], axis=0).T
    kernel, _, _ = pair(down, across, tail[VARIANCE : VARIANCE + 1, :], down[:, 4:5], live)
    same = iota((B, B), 0) == iota((B, B), 1)
    cov = kernel + jnp.where(same, live * tail[NUG : NUG + 1, :] + 1.0 - live, 0.0)
    tiles = inverse_factor([cov[8 * v : 8 * (v + 1)] for v in range(B // 8)])
    for v in range(B // 8):
        out_ref[8 * v : 8 * (v + 1), reps:] = tiles[v]
    hot = (jnp.broadcast_to(fine, (B, B)).T == iota((B, B), 1).astype(F32)).astype(BF16)
    out_ref[:HALF, :reps] = picked2(hot[:HALF], up[:reps, :])
    out_ref[HALF:B, :reps] = picked2(hot[HALF:], left[:reps, :])
    out_ref[B : 2 * B, :reps] = tile[:reps, :].T
    out_ref[B : 2 * B, reps:] = jnp.zeros((B, B), F32)


def first_kernel(table, given, out_ref, k_ref, s_ref, d_ref, u_ref, left_ref, right_ref, f_ref, f3_ref, y_ref):
    lines = given[2 * B :, : 2 * B]
    ends = given[2 * B :, 2 * B :]
    wanted = ends[1:2].astype(jnp.int32)
    tile_hot = (iota((B, COARSE), 0) == wanted // CP).astype(BF16)
    rows = picked(table[:, : 4 * CP], tile_hot, tn)
    rows = jnp.where((iota((4 * CP, COARSE), 0) % CP) == wanted % CP, rows, 0.0)
    across = []
    for k in range(4):
        line = jnp.sum(rows[k * CP : (k + 1) * CP], axis=0, keepdims=True) / ends[2 + k : 3 + k]
        across.append(jnp.concatenate([lines[k : k + 1, :B], line, lines[k : k + 1, B:]], axis=1))
    live = jnp.concatenate([lines[4:5, :B], jnp.ones((1, N - B), F32)], axis=1)
    down = jnp.concatenate(across + [live] + [jnp.zeros((B - 5, N), F32)], axis=0).T
    variance = jnp.concatenate([ends[6:7], ends[6:7, : N - COARSE]], axis=1)
    nugget = jnp.concatenate([ends[7:8], ends[7:8, : N - COARSE]], axis=1)
    out_ref[FIELDS : FIELDS + 2 * B, :LEAD] = given[: 2 * B, :LEAD]
    out_ref[FIELDS:, LEAD:] = jnp.broadcast_to(ends[0:1], (B, COARSE)).T
    for r in range(N // B):
        here = slice(r * B, (r + 1) * B)
        kernel, common, squares = pair(down[here], across, variance, down[here, 4:5], live)
        for i, part in enumerate([kernel] + [common * square for square in squares]):
            there = slice(i * N, (i + 1) * N)
            f_ref[here, there], f_ref[N + r * B : N + (r + 1) * B, there], f3_ref[here, there] = thirds(part)
        same = iota((B, N), 0) + r * B == iota((B, N), 1)
        k_ref[here, :] = kernel + jnp.where(same, live * nugget + 1.0 - live, 0.0)

    def conditional(p):
        at = pl.multiple_of(p * B, B)
        after = pl.multiple_of(p * B + B, B)
        u = nn(six_left(d_ref[...]), six_right(k_ref[pl.ds(at, B), pl.ds(after, B)]), None)
        s_ref[...] = k_ref[pl.ds(after, B), pl.ds(after, B)] - nn(six_left(u.T), six_right(u), None)

    d_ref[...] = given[:B, LEAD:]
    conditional(0)

    def sweep(p, carry):
        tiles = inverse_factor([s_ref[8 * v : 8 * (v + 1), :] for v in range(B // 8)])
        last = pl.multiple_of(p * B - B, B)
        d = d_ref[...]
        u_ref[...] = nn(six_left(d), six_right(k_ref[pl.ds(last, B), :]), None)
        u_ref[:, pl.ds(last, B)] = -d
        k_ref[pl.ds(last, B), :] = jnp.zeros((B, N), F32)
        k_ref[:, pl.ds(last, B)] = jnp.zeros((N, B), F32)
        left_ref[...] = six_left(u_ref[...].T)
        right_ref[...] = six_right(u_ref[...])
        k_ref[...] -= nn(left_ref[...], right_ref[...], None)
        for v in range(B // 8):
            d_ref[8 * v : 8 * (v + 1), :] = tiles[v]

        @pl.when(p < N // B - 1)
        def _():
            conditional(p)

        return carry

    lax.fori_loop(1, N // B, sweep, 0)
    d = d_ref[...]
    out_ref[MROW : MROW + B, :LEAD] = -nt(d, k_ref[:LEAD, LEAD:])
    out_ref[MROW : MROW + B, LEAD:] = d
    m = out_ref[MROW : MROW + B, :]
    parts = halves(m)
    twice = jnp.concatenate([jnp.concatenate([part, part], axis=1) for part in parts], axis=0)
    large = nn(twice, f_ref[...], None)
    small = large[B:] + nn(parts[0], f3_ref[...], None)
    for i in range(5):
        there = slice(i * N, (i + 1) * N)
        y_ref[i * B : (i + 1) * B, :] = large[:B, there] + small[:, there]
    y_ref[5 * B :, :] = m * (live * nugget)
    high, low = halves(y_ref[...])
    out_ref[:MROW, :LEAD] = -three_terms((high[:, :LEAD], low[:, :LEAD]), halves(k_ref[:LEAD, :LEAD]), nn)
    out_ref[:MROW, LEAD:] = three_terms((high, low), parts, nt)

    def folded(x):
        x = jnp.sum(x.reshape(B // 8, 8, x.shape[1]), axis=0)
        total = x[:, :B]
        for c in range(1, x.shape[1] // B):
            total = total + x[:, c * B : (c + 1) * B]
        return total

    sums = []
    for i in range(6):
        for j in range(i + 1):
            lead_part = out_ref[i * B : (i + 1) * B, :LEAD] * y_ref[j * B : (j + 1) * B, :LEAD]
            own_part = out_ref[i * B : (i + 1) * B, LEAD:] * out_ref[j * B : (j + 1) * B, LEAD:]
            sums.append(jnp.sum(2.0 * folded(lead_part) + folded(own_part), axis=0, keepdims=True))
    for i in range(6):
        sums.append(jnp.sum(folded(y_ref[i * B : (i + 1) * B, :] * m), axis=0, keepdims=True))
    sums.append(jnp.zeros((5, B), F32))
    out_ref[PROW:FIELDS, :B] = jnp.concatenate(sums, axis=0)


def picked2(one_hot, table):
    high, low = halves(table)
    return nt(one_hot, high, None) + nt(one_hot, low, None)


def second_kernel(arrived, given, white_ref, row_ref, v_ref):
    reps = white_ref.shape[0]
    chunks = reps // B
    held = arrived.shape[0] // chunks
    v_ref[:B, :] = given[FIELDS : FIELDS + B, :reps]
    v_ref[LEAD:, :] = given[FIELDS + B : FIELDS + 2 * B, :reps]
    hot = (given[FIELDS:, LEAD : LEAD + 1] == iota((COARSE, held), 1).astype(F32)).astype(BF16)
    for c in range(chunks):
        high, low = halves(arrived[pl.ds(c, held, stride=chunks), :])
        v_ref[B:LEAD, c * B : (c + 1) * B] = nn(hot, high, None) + nn(hot, low, None)
    white = nn(given[MROW : MROW + B, :], v_ref[...])
    white_ref[...] = white.T
    cross = nt(white, v_ref[:LEAD, :])
    square = nt(white, white)
    part = given[PROW:FIELDS, :B]
    lines = []
    for i in range(6):
        both = given[i * B : (i + 1) * B, :LEAD] * cross
        both = (both[:, :B] + both[:, B : 2 * B]) + (both[:, 2 * B : 3 * B] + both[:, 3 * B :])
        both = both + 0.5 * (given[i * B : (i + 1) * B, LEAD:] * square)
        lines.append(jnp.sum(both, axis=0, keepdims=True) - (0.5 * reps) * part[21 + i : 22 + i, :])
    whole = jnp.concatenate([(0.5 * reps) * part[:21, :]] + lines + [jnp.zeros((B - 27, B), F32)], axis=0)
    row_ref[...] = jnp.broadcast_to(jnp.sum(whole.T, axis=0, keepdims=True), row_ref.shape)


def third_kernel(rows, step_ref):
    total = jnp.broadcast_to(jnp.sum(rows[...], axis=0, keepdims=True), (8, B))
    sub, lane = iota((8, B), 0), iota((8, B), 1)
    a = jnp.zeros((8, B), F32)
    for i in range(6):
        for j in range(6):
            low, high = min(i, j), max(i, j)
            entry = jnp.broadcast_to(total[:, high * (high + 1) // 2 + low : high * (high + 1) // 2 + low + 1], (8, B))
            a = jnp.where((sub == i) & (lane == j), entry, a)
        entry = jnp.broadcast_to(total[:, 21 + i : 22 + i], (8, B))
        a = jnp.where((sub == i) & (lane == 6), entry, a)
    for k in range(6):
        row = jnp.broadcast_to(a[k : k + 1, :], (8, B))
        col = jnp.broadcast_to(a[:, k : k + 1], (8, B))
        row = row / jnp.broadcast_to(row[:, k : k + 1], (8, B))
        a = jnp.where(sub == k, row, a - col * row)
    step_ref[...] = jnp.sum(jnp.where((lane == sub) & (sub < 6), jnp.broadcast_to(a[:, 6:7], (8, B)), 0.0), axis=0)[:6]


def body(coords, values, coarse_coords, coarse_values, fine_index, coarse_index, log_params):
    reps = values.shape[0]
    devices = lax.axis_size("row") * lax.axis_size("col")
    vmem = pl.BlockSpec(memory_space=pltpu.VMEM)
    smem = pl.BlockSpec(memory_space=pltpu.SMEM)

    def shape(*dims):
        return jax.ShapeDtypeStruct(dims, F32)

    def cost(flops):
        return pl.CostEstimate(flops=flops, bytes_accessed=2**20, transcendentals=0)

    def room(mib):
        return pltpu.CompilerParams(vmem_limit_bytes=mib * 2**20)

    request, tile = pl.pallas_call(
        request_kernel,
        out_shape=(shape(devices, B), shape(reps + TAIL, B)),
        in_specs=[smem] + [vmem] * 5,
        out_specs=(vmem,) * 2,
        compiler_params=room(60),
        name="request_part",
    )(log_params, coarse_coords, coarse_index, coords, values, fine_index)
    up = shifted(tile, "row", 1)
    left = passed_along(tile, "col", 1)
    table = lax.all_to_all(request, AXES, 0, 0, tiled=True)
    fine = pl.pallas_call(
        fine_kernel,
        out_shape=shape(2 * B + 8, N),
        in_specs=[vmem] * 3,
        out_specs=vmem,
        compiler_params=room(8),
        cost_estimate=cost(4 * 10**9),
        name="fine_part",
    )(tile, up, left)
    send = pl.pallas_call(
        send_kernel,
        out_shape=shape(devices * MOST * reps // B, B),
        in_specs=[vmem] * 2 + [pl.BlockSpec(memory_space=pl.ANY)],
        out_specs=vmem,
        compiler_params=room(8),
        name="send_part",
    )(table, coarse_values.T, fine)
    arrived = lax.all_to_all(send, AXES, 0, 0, tiled=True)
    parts = pl.pallas_call(
        first_kernel,
        out_shape=shape(FIELDS + COARSE, N),
        in_specs=[vmem] * 2,
        out_specs=vmem,
        scratch_shapes=[
            pltpu.VMEM((N, N), F32),
            pltpu.VMEM((B, B), F32),
            pltpu.VMEM((B, B), F32),
            pltpu.VMEM((B, N), F32),
            pltpu.VMEM((N, 6 * B), BF16),
            pltpu.VMEM((6 * B, N), BF16),
            pltpu.VMEM((2 * N, 5 * N), BF16),
            pltpu.VMEM((N, 5 * N), BF16),
            pltpu.VMEM((6 * B, N), F32),
        ],
        compiler_params=room(36),
        cost_estimate=cost(30 * 10**9),
        name="fisher_part",
    )(table, fine)
    white, row = pl.pallas_call(
        second_kernel,
        out_shape=(shape(reps, B), shape(devices, B)),
        in_specs=[vmem] * 2,
        out_specs=(vmem,) * 2,
        scratch_shapes=[pltpu.VMEM((N, reps), F32)],
        compiler_params=room(24),
        name="gradient_part",
    )(arrived, parts)
    rows = lax.all_to_all(row, AXES, 0, 0, tiled=True)
    step = pl.pallas_call(
        third_kernel,
        out_shape=shape(6),
        in_specs=[vmem],
        out_specs=vmem,
        compiler_params=room(8),
        name="solve_part",
    )(rows)
    return (step, white)


def solution(mesh):
    in_specs = (
        P(None, AXES),
        P(None, AXES),
        P(None, AXES),
        P(None, AXES),
        P(AXES, None),
        P(AXES, None),
        P(),
    )
    out_specs = (P(), P(None, AXES))
    return jax.shard_map(body, mesh=mesh, in_specs=in_specs, out_specs=out_specs, check_vma=False)
```

```python
import math

import jax
import jax.numpy as jnp
from jax import lax
from jax.experimental import pallas as pl
from jax.experimental.pallas import tpu as pltpu
from jax.sharding import PartitionSpec as P

HIGH = lax.Precision.HIGHEST
ROOT_FIVE = math.sqrt(5.0)
NUGGET = 0.2
RANGE_BASE = 0.5
F32 = jnp.float32
BF16 = jnp.bfloat16
AXES = ("row", "col")

B = 128
N = 640
LEAD = 512
COARSE = 384
HALF = 64
CP = 16
MOST = 6
FINE, PLACE, WANTED, SPREAD, VARIANCE, NUG, TAIL = 4, 5, 8, 11, 15, 16, 24
MROW, PROW, TOTAL_ROWS = 640, 768, 776


def shifted(value, axis, steps):
    count = lax.axis_size(axis)
    first, last = (max(0, -steps), min(count, count - steps))
    return lax.ppermute(value, axis, [(source, source + steps) for source in range(first, last)])


def passed_along(block, axis, distance):
    devices = range(lax.axis_size(axis))
    route = [((i - distance) % len(devices), i) for i in devices]
    return lax.ppermute(block, axis, route)


def nn(a, b, precision=HIGH):
    return lax.dot_general(a, b, (((1,), (0,)), ((), ())), precision=precision, preferred_element_type=F32)


def nt(a, b, precision=HIGH):
    return lax.dot_general(a, b, (((1,), (1,)), ((), ())), precision=precision, preferred_element_type=F32)


def tn(a, b, precision=HIGH):
    return lax.dot_general(a, b, (((0,), (0,)), ((), ())), precision=precision, preferred_element_type=F32)


def iota(shape, dim):
    return lax.broadcasted_iota(jnp.int32, shape, dim)


def halves(x):
    high = x.astype(BF16)
    return high, (x - high.astype(F32)).astype(BF16)


def thirds(x):
    high = x.astype(BF16)
    rest = x - high.astype(F32)
    mid = rest.astype(BF16)
    return high, mid, (rest - mid.astype(F32)).astype(BF16)


def picked(table, one_hot, dot):
    high, mid, low = thirds(table)
    return (dot(high, one_hot, None) + dot(mid, one_hot, None)) + dot(low, one_hot, None)


def six_left(x):
    one, two, three = thirds(x)
    return jnp.concatenate([one, one, two, two, one, three], axis=1)


def six_right(x):
    one, two, three = thirds(x)
    return jnp.concatenate([one, two, one, two, three, one], axis=0)


def three_terms(left, right, dot):
    rows = left[0].shape[0]
    both = dot(jnp.concatenate(left, axis=0), right[0], None)
    return (both[:rows] + both[rows:]) + dot(left[0], right[1], None)


def wide(x, j):
    return jnp.broadcast_to(x[:, j : j + 1], (8, B))


def tall(x, k):
    return jnp.broadcast_to(x[k : k + 1, :], (8, B))


def inverse_factor(s):
    tiles = B // 8
    s = list(s)
    sub, lane = iota((8, B), 0), iota((8, B), 1)
    out = []
    ahead = [wide(s[0], j) for j in range(8)]
    for g in range(tiles):
        k0 = 8 * g
        more = g + 1 < tiles
        cols = ahead
        inside = (lane >= k0) & (lane < k0 + 8)
        mine = jnp.where(inside, (lane == sub + k0).astype(F32), s[g])
        if more:
            near = [wide(s[g + 1], k0 + j) for j in range(8)]
            ahead = [wide(s[g + 1], k0 + 8 + j) for j in range(8)]
            after = jnp.where(inside, 0.0, s[g + 1])
        pivots = jnp.ones((8, B), F32)
        pivot = tall(cols[0], 0)
        scaled, rows = [], []
        for k in range(8):
            pivots = jnp.where(sub == k, pivot, pivots)
            over = 1.0 / pivot
            at = [tall(cols[k], later) for later in range(k + 1, 8)]
            if k < 7:
                pivot = tall(cols[k + 1], k + 1) - (at[0] * at[0]) * over
            at = [entry * over for entry in at]
            row = tall(mine, k) * over
            column = jnp.where(sub > k, cols[k], 0.0)
            for later in range(k + 1, 8):
                cols[later] = cols[later] - column * at[later - k - 1]
            mine = mine - column * row
            scaled.append(at)
            rows.append(row)
            if more:
                for later in range(k + 1, 8):
                    near[later] = near[later] - near[k] * at[later - k - 1]
                for j in range(8):
                    ahead[j] = ahead[j] - near[k] * (tall(near[k], j) * over)
                after = after - near[k] * row
        if more:
            s[g + 1] = after
        for v in range(g + 2, tiles):
            col = [wide(s[v], k0 + j) for j in range(8)]
            x = jnp.where(inside, 0.0, s[v])
            for k in range(8):
                for later in range(k + 1, 8):
                    col[later] = col[later] - col[k] * scaled[k][later - k - 1]
                x = x - col[k] * rows[k]
            s[v] = x
        root = lax.rsqrt(pivots)
        root = root * (1.5 - 0.5 * pivots * root * root)
        out.append(jnp.where(lane <= sub + k0, mine * root, 0.0))
    return out


def request_kernel(theta, coarse_coords, coarse, coords, values, fine, out_ref, tile_ref):
    reps = values.shape[0]
    tile, slot = coarse[...] // CP, coarse[...] % CP
    hot = (iota((B, COARSE), 0) == tile).astype(BF16)
    earlier = (iota((COARSE, COARSE), 0) < iota((COARSE, COARSE), 1)).astype(BF16)
    rank = jnp.sum(hot.astype(F32) * nn(hot, earlier, None), axis=0, keepdims=True).astype(jnp.int32)
    asked = jnp.where(iota((B, COARSE), 0) == rank + 4 * CP, slot, 0).astype(F32).astype(BF16)
    line = jnp.concatenate([coarse_coords[k : k + 1, :] for k in range(4)] + [jnp.zeros((1, B - 4 * CP), F32)], axis=1)
    out_ref[...] = line + nt(hot, asked, None)
    place = (tile * MOST + rank).astype(F32)
    wanted = coarse[...].astype(F32)
    rows = [coords[...], fine[...].astype(F32)]
    rows += [place[:, c * B : (c + 1) * B] for c in range(COARSE // B)]
    rows += [wanted[:, c * B : (c + 1) * B] for c in range(COARSE // B)]
    rows += [jnp.exp(jnp.full((1, B), theta[1 + k], F32)) * RANGE_BASE for k in range(4)]
    rows += [jnp.exp(jnp.full((1, B), theta[0], F32)), NUGGET * jnp.exp(jnp.full((1, B), theta[5], F32))]
    rows += [jnp.zeros((TAIL - NUG - 1, B), F32)]
    tile_ref[:reps, :] = values[...]
    tile_ref[reps:, :] = jnp.concatenate(rows, axis=0)


def send_kernel(table, coarse_values, after, send_ref):
    del after
    three = jnp.concatenate(thirds(coarse_values[...]), axis=0)
    slots = (iota((B, 3 * CP), 1) % CP).astype(F32)
    chunks = coarse_values.shape[1] // B
    for r in range(MOST):
        hot = (table[:, 4 * CP + r : 4 * CP + r + 1] == slots).astype(BF16)
        rows = nn(hot, three, None)
        for c in range(chunks):
            send_ref[pl.ds(r * chunks + c, B, stride=MOST * chunks), :] = rows[:, c * B : (c + 1) * B]


def pair(down, across, variance, live_down, live_across):
    squares = []
    for k in range(4):
        gap = down[:, k : k + 1] - across[k]
        squares.append(gap * gap)
    root = ROOT_FIVE * jnp.sqrt((squares[0] + squares[1]) + (squares[2] + squares[3]))
    paired = (live_down * live_across) * (variance * jnp.exp(-root))
    return paired * (1.0 + root + root * root * (1.0 / 3.0)), paired * ((5.0 / 3.0) * (1.0 + root)), squares


def fine_kernel(tile, up, left, out_ref):
    reps = tile.shape[0] - TAIL
    tail = tile[reps:, :]
    fine = tail[FINE : FINE + 1, :]
    column = iota((B, HALF), 0).astype(F32)
    up_hot = (column == fine[:, :HALF]).astype(BF16)
    left_hot = (column == fine[:, HALF:]).astype(BF16)
    upper_live = (lax.axis_index("row") > 0).astype(F32)
    picks = jnp.concatenate(
        [picked(up[reps : reps + 8, :], up_hot, nn) * upper_live, picked(left[reps : reps + 8, :], left_hot, nn)], axis=1
    )
    across = [picks[k : k + 1] / tail[SPREAD + k : SPREAD + k + 1] for k in range(4)]
    live = jnp.where(iota((1, B), 1) < HALF, upper_live, 1.0)
    lines = jnp.concatenate(across + [live, jnp.zeros((3, B), F32)], axis=0)
    own_lines = [tail[k : k + 1, :] / tail[SPREAD + k : SPREAD + k + 1] for k in range(4)]
    own_lines = jnp.concatenate(own_lines + [jnp.ones((1, B), F32), jnp.zeros((3, B), F32)], axis=0)
    thrice = jnp.concatenate([tail[SPREAD : NUG + 1, :]] * 3, axis=1)
    ends = [jnp.concatenate([tail[n + c : n + c + 1, :] for c in range(3)], axis=1) for n in (PLACE, WANTED)]
    out_ref[2 * B :, :] = jnp.concatenate([lines, own_lines, jnp.concatenate(ends + [thrice], axis=0)], axis=1)
    down = jnp.concatenate([lines, jnp.zeros((B - 8, B), F32)], axis=0).T
    kernel, _, _ = pair(down, across, tail[VARIANCE : VARIANCE + 1, :], down[:, 4:5], live)
    same = iota((B, B), 0) == iota((B, B), 1)
    cov = kernel + jnp.where(same, live * tail[NUG : NUG + 1, :] + 1.0 - live, 0.0)
    tiles = inverse_factor([cov[8 * v : 8 * (v + 1)] for v in range(B // 8)])
    for v in range(B // 8):
        out_ref[8 * v : 8 * (v + 1), reps:] = tiles[v]
    hot = (jnp.broadcast_to(fine, (B, B)).T == iota((B, B), 1).astype(F32)).astype(BF16)
    out_ref[:HALF, :reps] = picked2(hot[:HALF], up[:reps, :])
    out_ref[HALF:B, :reps] = picked2(hot[HALF:], left[:reps, :])
    out_ref[B : 2 * B, :reps] = tile[:reps, :].T
    out_ref[B : 2 * B, reps:] = jnp.zeros((B, B), F32)


def first_kernel(table, given, out_ref, k_ref, s_ref, d_ref, u_ref, left_ref, right_ref, f_ref, f3_ref, y_ref):
    lines = given[2 * B :, : 2 * B]
    ends = given[2 * B :, 2 * B :]
    wanted = ends[1:2].astype(jnp.int32)
    tile_hot = (iota((B, COARSE), 0) == wanted // CP).astype(BF16)
    rows = picked(table[:, : 4 * CP], tile_hot, tn)
    rows = jnp.where((iota((4 * CP, COARSE), 0) % CP) == wanted % CP, rows, 0.0)
    across = []
    for k in range(4):
        line = jnp.sum(rows[k * CP : (k + 1) * CP], axis=0, keepdims=True) / ends[2 + k : 3 + k]
        across.append(jnp.concatenate([lines[k : k + 1, :B], line, lines[k : k + 1, B:]], axis=1))
    live = jnp.concatenate([lines[4:5, :B], jnp.ones((1, N - B), F32)], axis=1)
    down = jnp.concatenate(across + [live] + [jnp.zeros((B - 5, N), F32)], axis=0).T
    variance = jnp.concatenate([ends[6:7], ends[6:7, : N - COARSE]], axis=1)
    nugget = jnp.concatenate([ends[7:8], ends[7:8, : N - COARSE]], axis=1)
    for r in range(N // B):
        here = slice(r * B, (r + 1) * B)
        kernel, common, squares = pair(down[here], across, variance, down[here, 4:5], live)
        for i, part in enumerate([common * square for square in squares]):
            there = slice(i * N, (i + 1) * N)
            f_ref[here, there], f_ref[N + r * B : N + (r + 1) * B, there], f3_ref[here, there] = thirds(part)
        same = iota((B, N), 0) + r * B == iota((B, N), 1)
        k_ref[here, :] = kernel + jnp.where(same, live * nugget + 1.0 - live, 0.0)

    def conditional(p):
        at = pl.multiple_of(p * B, B)
        after = pl.multiple_of(p * B + B, B)
        u = nn(six_left(d_ref[...]), six_right(k_ref[pl.ds(at, B), pl.ds(after, B)]), None)
        s_ref[...] = k_ref[pl.ds(after, B), pl.ds(after, B)] - nn(six_left(u.T), six_right(u), None)

    d_ref[...] = given[:B, LEAD:]
    conditional(0)

    def sweep(p, carry):
        tiles = inverse_factor([s_ref[8 * v : 8 * (v + 1), :] for v in range(B // 8)])
        last = pl.multiple_of(p * B - B, B)
        d = d_ref[...]
        u_ref[...] = nn(six_left(d), six_right(k_ref[pl.ds(last, B), :]), None)
        u_ref[:, pl.ds(last, B)] = -d
        k_ref[pl.ds(last, B), :] = jnp.zeros((B, N), F32)
        k_ref[:, pl.ds(last, B)] = jnp.zeros((N, B), F32)
        left_ref[...] = six_left(u_ref[...].T)
        right_ref[...] = six_right(u_ref[...])
        k_ref[...] -= nn(left_ref[...], right_ref[...], None)
        for v in range(B // 8):
            d_ref[8 * v : 8 * (v + 1), :] = tiles[v]

        @pl.when(p < N // B - 1)
        def _():
            conditional(p)

        return carry

    lax.fori_loop(1, N // B, sweep, 0)
    d = d_ref[...]
    out_ref[MROW : MROW + B, :LEAD] = -nt(d, k_ref[:LEAD, LEAD:])
    out_ref[MROW : MROW + B, LEAD:] = d
    m = out_ref[MROW : MROW + B, :]
    parts = halves(m)
    twice = jnp.concatenate([jnp.concatenate([part, part], axis=1) for part in parts], axis=0)
    large = nn(twice, f_ref[...], None)
    small = large[B:] + nn(parts[0], f3_ref[...], None)
    y_ref[:B, :] = m * (live * nugget)
    for i in range(4):
        there = slice(i * N, (i + 1) * N)
        y_ref[(i + 1) * B : (i + 2) * B, :] = large[:B, there] + small[:, there]
    high, low = halves(y_ref[...])
    out_ref[:MROW, :LEAD] = -three_terms((high[:, :LEAD], low[:, :LEAD]), halves(k_ref[:LEAD, :LEAD]), nn)
    out_ref[:MROW, LEAD:] = three_terms((high, low), parts, nt)

    def folded(x):
        x = jnp.sum(x.reshape(B // 8, 8, x.shape[1]), axis=0)
        total = x[:, :B]
        for c in range(1, x.shape[1] // B):
            total = total + x[:, c * B : (c + 1) * B]
        return total

    def z_of(i):
        return out_ref[i * B : (i + 1) * B, :LEAD]

    def g_of(i):
        return out_ref[i * B : (i + 1) * B, LEAD:]

    def line(x):
        return jnp.sum(x, axis=0, keepdims=True)

    eye = (iota((B, B), 0) == iota((B, B), 1)).astype(F32)
    pairs, traces = {}, [line(folded(g_of(i) * eye)) for i in range(5)]
    for i in range(5):
        for j in range(i + 1):
            lead_part = z_of(i) * y_ref[j * B : (j + 1) * B, :LEAD]
            pairs[i, j] = line(2.0 * folded(lead_part) + folded(g_of(i) * g_of(j)))
    ones = jnp.ones((1, B), F32)
    sums = [pairs[0, 0] + (ones - 2.0 * traces[0])]
    for i in range(1, 5):
        sums += [traces[i] - pairs[i, 0]] + [pairs[i, j] for j in range(1, i + 1)]
    sums += [traces[0] - pairs[0, 0]] + [pairs[j, 0] for j in range(1, 5)] + [pairs[0, 0]]
    sums += [ones - traces[0]] + traces[1:] + [traces[0]]
    sums.append(jnp.zeros((B - 27, B), F32))
    out_ref[PROW:, :B] = jnp.broadcast_to(line(jnp.concatenate(sums, axis=0).T), (8, B))


def picked2(one_hot, table):
    high, low = halves(table)
    return nt(one_hot, high, None) + nt(one_hot, low, None)


def second_kernel(arrived, given, fine, white_ref, row_ref, v_ref):
    reps = white_ref.shape[0]
    chunks = reps // B
    held = arrived.shape[0] // chunks
    v_ref[:B, :] = fine[:B, :reps]
    v_ref[LEAD:, :] = fine[B : 2 * B, :reps]
    place = jnp.broadcast_to(fine[2 * B : 2 * B + 1, 2 * B :], (B, COARSE)).T[:, :1]
    hot = (place == iota((COARSE, held), 1).astype(F32)).astype(BF16)
    for c in range(chunks):
        high, low = halves(arrived[pl.ds(c, held, stride=chunks), :])
        v_ref[B:LEAD, c * B : (c + 1) * B] = nn(hot, high, None) + nn(hot, low, None)
    white = nn(given[MROW : MROW + B, :], v_ref[...])
    white_ref[...] = white.T
    cross = nt(white, v_ref[:LEAD, :])
    square = nt(white, white)
    eye = (iota((B, B), 0) == iota((B, B), 1)).astype(F32)
    leads, owns = [], []
    for i in range(5):
        both = given[i * B : (i + 1) * B, :LEAD] * cross
        leads.append((both[:, :B] + both[:, B : 2 * B]) + (both[:, 2 * B : 3 * B] + both[:, 3 * B :]))
        owns.append(0.5 * (given[i * B : (i + 1) * B, LEAD:] * square))
    terms = [0.5 * (eye * square) - owns[0] - leads[0]] + [leads[i] + owns[i] for i in (1, 2, 3, 4, 0)]
    terms = [jnp.sum(term, axis=0, keepdims=True) for term in terms]
    whole = jnp.concatenate([jnp.zeros((21, B), F32)] + terms + [jnp.zeros((B - 27, B), F32)], axis=0)
    weight = jnp.where(iota((1, B), 1) < 21, 0.5 * reps, -0.5 * reps)
    row = jnp.sum(whole.T, axis=0, keepdims=True) + weight * given[PROW : PROW + 1, :B]
    row_ref[...] = jnp.broadcast_to(row, row_ref.shape)


def third_kernel(rows, step_ref):
    total = jnp.broadcast_to(jnp.sum(rows[...], axis=0, keepdims=True), (8, B))
    sub, lane = iota((8, B), 0), iota((8, B), 1)
    a = jnp.zeros((8, B), F32)
    for i in range(6):
        for j in range(6):
            low, high = min(i, j), max(i, j)
            entry = jnp.broadcast_to(total[:, high * (high + 1) // 2 + low : high * (high + 1) // 2 + low + 1], (8, B))
            a = jnp.where((sub == i) & (lane == j), entry, a)
        entry = jnp.broadcast_to(total[:, 21 + i : 22 + i], (8, B))
        a = jnp.where((sub == i) & (lane == 6), entry, a)
    for k in range(6):
        row = jnp.broadcast_to(a[k : k + 1, :], (8, B))
        col = jnp.broadcast_to(a[:, k : k + 1], (8, B))
        row = row / jnp.broadcast_to(row[:, k : k + 1], (8, B))
        a = jnp.where(sub == k, row, a - col * row)
    step_ref[...] = jnp.sum(jnp.where((lane == sub) & (sub < 6), jnp.broadcast_to(a[:, 6:7], (8, B)), 0.0), axis=0)[:6]


def body(coords, values, coarse_coords, coarse_values, fine_index, coarse_index, log_params):
    reps = values.shape[0]
    devices = lax.axis_size("row") * lax.axis_size("col")
    vmem = pl.BlockSpec(memory_space=pltpu.VMEM)
    smem = pl.BlockSpec(memory_space=pltpu.SMEM)

    def shape(*dims):
        return jax.ShapeDtypeStruct(dims, F32)

    def cost(flops):
        return pl.CostEstimate(flops=flops, bytes_accessed=2**20, transcendentals=0)

    def room(mib):
        return pltpu.CompilerParams(vmem_limit_bytes=mib * 2**20)

    request, tile = pl.pallas_call(
        request_kernel,
        out_shape=(shape(devices, B), shape(reps + TAIL, B)),
        in_specs=[smem] + [vmem] * 5,
        out_specs=(vmem,) * 2,
        compiler_params=room(60),
        name="request_part",
    )(log_params, coarse_coords, coarse_index, coords, values, fine_index)
    up = shifted(tile, "row", 1)
    left = passed_along(tile, "col", 1)
    table = lax.all_to_all(request, AXES, 0, 0, tiled=True)
    fine = pl.pallas_call(
        fine_kernel,
        out_shape=shape(2 * B + 8, N),
        in_specs=[vmem] * 3,
        out_specs=vmem,
        compiler_params=room(8),
        cost_estimate=cost(4 * 10**9),
        name="fine_part",
    )(tile, up, left)
    send = pl.pallas_call(
        send_kernel,
        out_shape=shape(devices * MOST * reps // B, B),
        in_specs=[vmem] * 2 + [pl.BlockSpec(memory_space=pl.ANY)],
        out_specs=vmem,
        compiler_params=room(8),
        name="send_part",
    )(table, coarse_values.T, fine)
    arrived = lax.all_to_all(send, AXES, 0, 0, tiled=True)
    parts = pl.pallas_call(
        first_kernel,
        out_shape=shape(TOTAL_ROWS, N),
        in_specs=[vmem] * 2,
        out_specs=vmem,
        scratch_shapes=[
            pltpu.VMEM((N, N), F32),
            pltpu.VMEM((B, B), F32),
            pltpu.VMEM((B, B), F32),
            pltpu.VMEM((B, N), F32),
            pltpu.VMEM((N, 6 * B), BF16),
            pltpu.VMEM((6 * B, N), BF16),
            pltpu.VMEM((2 * N, 4 * N), BF16),
            pltpu.VMEM((N, 4 * N), BF16),
            pltpu.VMEM((5 * B, N), F32),
        ],
        compiler_params=room(36),
        cost_estimate=cost(30 * 10**9),
        name="fisher_part",
    )(table, fine)
    white, row = pl.pallas_call(
        second_kernel,
        out_shape=(shape(reps, B), shape(devices, B)),
        in_specs=[vmem] * 3,
        out_specs=(vmem,) * 2,
        scratch_shapes=[pltpu.VMEM((N, reps), F32)],
        compiler_params=room(24),
        name="gradient_part",
    )(arrived, parts, fine)
    rows = lax.all_to_all(row, AXES, 0, 0, tiled=True)
    step = pl.pallas_call(
        third_kernel,
        out_shape=shape(6),
        in_specs=[vmem],
        out_specs=vmem,
        compiler_params=room(8),
        name="solve_part",
    )(rows)
    return (step, white)


def solution(mesh):
    in_specs = (
        P(None, AXES),
        P(None, AXES),
        P(None, AXES),
        P(None, AXES),
        P(AXES, None),
        P(AXES, None),
        P(),
    )
    out_specs = (P(), P(None, AXES))
    return jax.shard_map(body, mesh=mesh, in_specs=in_specs, out_specs=out_specs, check_vma=False)
```

```python
import math

import jax
import jax.numpy as jnp
from jax import lax
from jax.experimental import pallas as pl
from jax.experimental.pallas import tpu as pltpu
from jax.sharding import PartitionSpec as P

HIGH = lax.Precision.HIGHEST
ROOT_FIVE = math.sqrt(5.0)
NUGGET = 0.2
RANGE_BASE = 0.5
F32 = jnp.float32
BF16 = jnp.bfloat16
AXES = ("row", "col")

B = 128
N = 640
LEAD = 512
COARSE = 384
HALF = 64
CP = 16
MOST = 6
FINE, PLACE, WANTED, SPREAD, VARIANCE, NUG, TAIL = 4, 5, 8, 11, 15, 16, 24
MROW, PROW, TOTAL_ROWS = 640, 768, 776


def shifted(value, axis, steps):
    count = lax.axis_size(axis)
    first, last = (max(0, -steps), min(count, count - steps))
    return lax.ppermute(value, axis, [(source, source + steps) for source in range(first, last)])


def passed_along(block, axis, distance):
    devices = range(lax.axis_size(axis))
    route = [((i - distance) % len(devices), i) for i in devices]
    return lax.ppermute(block, axis, route)


def nn(a, b, precision=HIGH):
    return lax.dot_general(a, b, (((1,), (0,)), ((), ())), precision=precision, preferred_element_type=F32)


def nt(a, b, precision=HIGH):
    return lax.dot_general(a, b, (((1,), (1,)), ((), ())), precision=precision, preferred_element_type=F32)


def tn(a, b, precision=HIGH):
    return lax.dot_general(a, b, (((0,), (0,)), ((), ())), precision=precision, preferred_element_type=F32)


def iota(shape, dim):
    return lax.broadcasted_iota(jnp.int32, shape, dim)


def halves(x):
    high = x.astype(BF16)
    return high, (x - high.astype(F32)).astype(BF16)


def thirds(x):
    high = x.astype(BF16)
    rest = x - high.astype(F32)
    mid = rest.astype(BF16)
    return high, mid, (rest - mid.astype(F32)).astype(BF16)


def picked(table, one_hot, dot):
    high, mid, low = thirds(table)
    return (dot(high, one_hot, None) + dot(mid, one_hot, None)) + dot(low, one_hot, None)


def six_left(x):
    one, two, three = thirds(x)
    return jnp.concatenate([one, one, two, two, one, three], axis=1)


def six_right(x):
    one, two, three = thirds(x)
    return jnp.concatenate([one, two, one, two, three, one], axis=0)


def three_terms(left, right, dot):
    rows = left[0].shape[0]
    both = dot(jnp.concatenate(left, axis=0), right[0], None)
    return (both[:rows] + both[rows:]) + dot(left[0], right[1], None)


def wide(x, j):
    return jnp.broadcast_to(x[:, j : j + 1], (8, B))


def tall(x, k):
    return jnp.broadcast_to(x[k : k + 1, :], (8, B))


def inverse_factor(s):
    tiles = B // 8
    s = list(s)
    sub, lane = iota((8, B), 0), iota((8, B), 1)
    out = []
    ahead = [wide(s[0], j) for j in range(8)]
    for g in range(tiles):
        k0 = 8 * g
        more = g + 1 < tiles
        cols = ahead
        inside = (lane >= k0) & (lane < k0 + 8)
        mine = jnp.where(inside, (lane == sub + k0).astype(F32), s[g])
        if more:
            near = [wide(s[g + 1], k0 + j) for j in range(8)]
            ahead = [wide(s[g + 1], k0 + 8 + j) for j in range(8)]
            after = jnp.where(inside, 0.0, s[g + 1])
        pivots = jnp.ones((8, B), F32)
        pivot = tall(cols[0], 0)
        scaled, rows = [], []
        for k in range(8):
            pivots = jnp.where(sub == k, pivot, pivots)
            over = 1.0 / pivot
            at = [tall(cols[k], later) for later in range(k + 1, 8)]
            if k < 7:
                pivot = tall(cols[k + 1], k + 1) - (at[0] * at[0]) * over
            at = [entry * over for entry in at]
            row = tall(mine, k) * over
            column = jnp.where(sub > k, cols[k], 0.0)
            for later in range(k + 1, 8):
                cols[later] = cols[later] - column * at[later - k - 1]
            mine = mine - column * row
            scaled.append(at)
            rows.append(row)
            if more:
                for later in range(k + 1, 8):
                    near[later] = near[later] - near[k] * at[later - k - 1]
                for j in range(8):
                    ahead[j] = ahead[j] - near[k] * (tall(near[k], j) * over)
                after = after - near[k] * row
        if more:
            s[g + 1] = after
        for v in range(g + 2, tiles):
            col = [wide(s[v], k0 + j) for j in range(8)]
            x = jnp.where(inside, 0.0, s[v])
            for k in range(8):
                for later in range(k + 1, 8):
                    col[later] = col[later] - col[k] * scaled[k][later - k - 1]
                x = x - col[k] * rows[k]
            s[v] = x
        root = lax.rsqrt(pivots)
        root = root * (1.5 - 0.5 * pivots * root * root)
        out.append(jnp.where(lane <= sub + k0, mine * root, 0.0))
    return out


def request_kernel(theta, coarse_coords, coarse, coords, values, fine, out_ref, tile_ref):
    reps = values.shape[0]
    tile, slot = coarse[...] // CP, coarse[...] % CP
    hot = (iota((B, COARSE), 0) == tile).astype(BF16)
    earlier = (iota((COARSE, COARSE), 0) < iota((COARSE, COARSE), 1)).astype(BF16)
    rank = jnp.sum(hot.astype(F32) * nn(hot, earlier, None), axis=0, keepdims=True).astype(jnp.int32)
    asked = jnp.where(iota((B, COARSE), 0) == rank + 4 * CP, slot, 0).astype(F32).astype(BF16)
    line = jnp.concatenate([coarse_coords[k : k + 1, :] for k in range(4)] + [jnp.zeros((1, B - 4 * CP), F32)], axis=1)
    out_ref[...] = line + nt(hot, asked, None)
    place = (tile * MOST + rank).astype(F32)
    wanted = coarse[...].astype(F32)
    rows = [coords[...], fine[...].astype(F32)]
    rows += [place[:, c * B : (c + 1) * B] for c in range(COARSE // B)]
    rows += [wanted[:, c * B : (c + 1) * B] for c in range(COARSE // B)]
    rows += [jnp.exp(jnp.full((1, B), theta[1 + k], F32)) * RANGE_BASE for k in range(4)]
    rows += [jnp.exp(jnp.full((1, B), theta[0], F32)), NUGGET * jnp.exp(jnp.full((1, B), theta[5], F32))]
    rows += [jnp.zeros((TAIL - NUG - 1, B), F32)]
    tile_ref[:reps, :] = values[...]
    tile_ref[reps:, :] = jnp.concatenate(rows, axis=0)


def send_kernel(table, coarse_values, after, send_ref):
    del after
    three = jnp.concatenate(thirds(coarse_values[...]), axis=0)
    slots = (iota((B, 3 * CP), 1) % CP).astype(F32)
    chunks = coarse_values.shape[1] // B
    for r in range(MOST):
        hot = (table[:, 4 * CP + r : 4 * CP + r + 1] == slots).astype(BF16)
        rows = nn(hot, three, None)
        for c in range(chunks):
            send_ref[pl.ds(r * chunks + c, B, stride=MOST * chunks), :] = rows[:, c * B : (c + 1) * B]


def pair(down, across, variance, live_down, live_across):
    squares = []
    for k in range(4):
        gap = down[:, k : k + 1] - across[k]
        squares.append(gap * gap)
    root = ROOT_FIVE * jnp.sqrt((squares[0] + squares[1]) + (squares[2] + squares[3]))
    paired = (live_down * live_across) * (variance * jnp.exp(-root))
    return paired * (1.0 + root + root * root * (1.0 / 3.0)), paired * ((5.0 / 3.0) * (1.0 + root)), squares


def fine_kernel(tile, up, left, out_ref):
    reps = tile.shape[0] - TAIL
    tail = tile[reps:, :]
    fine = tail[FINE : FINE + 1, :]
    column = iota((B, HALF), 0).astype(F32)
    up_hot = (column == fine[:, :HALF]).astype(BF16)
    left_hot = (column == fine[:, HALF:]).astype(BF16)
    upper_live = (lax.axis_index("row") > 0).astype(F32)
    picks = jnp.concatenate(
        [picked(up[reps : reps + 8, :], up_hot, nn) * upper_live, picked(left[reps : reps + 8, :], left_hot, nn)], axis=1
    )
    across = [picks[k : k + 1] / tail[SPREAD + k : SPREAD + k + 1] for k in range(4)]
    live = jnp.where(iota((1, B), 1) < HALF, upper_live, 1.0)
    lines = jnp.concatenate(across + [live, jnp.zeros((3, B), F32)], axis=0)
    own_lines = [tail[k : k + 1, :] / tail[SPREAD + k : SPREAD + k + 1] for k in range(4)]
    own_lines = jnp.concatenate(own_lines + [jnp.ones((1, B), F32), jnp.zeros((3, B), F32)], axis=0)
    thrice = jnp.concatenate([tail[SPREAD : NUG + 1, :]] * 3, axis=1)
    ends = [jnp.concatenate([tail[n + c : n + c + 1, :] for c in range(3)], axis=1) for n in (PLACE, WANTED)]
    out_ref[2 * B :, :] = jnp.concatenate([lines, own_lines, jnp.concatenate(ends + [thrice], axis=0)], axis=1)
    down = jnp.concatenate([lines, jnp.zeros((B - 8, B), F32)], axis=0).T
    kernel, _, _ = pair(down, across, tail[VARIANCE : VARIANCE + 1, :], down[:, 4:5], live)
    same = iota((B, B), 0) == iota((B, B), 1)
    cov = kernel + jnp.where(same, live * tail[NUG : NUG + 1, :] + 1.0 - live, 0.0)
    tiles = inverse_factor([cov[8 * v : 8 * (v + 1)] for v in range(B // 8)])
    for v in range(B // 8):
        out_ref[8 * v : 8 * (v + 1), reps:] = tiles[v]
    hot = (jnp.broadcast_to(fine, (B, B)).T == iota((B, B), 1).astype(F32)).astype(BF16)
    out_ref[:HALF, :reps] = picked2(hot[:HALF], up[:reps, :])
    out_ref[HALF:B, :reps] = picked2(hot[HALF:], left[:reps, :])
    out_ref[B : 2 * B, :reps] = tile[:reps, :].T
    out_ref[B : 2 * B, reps:] = jnp.zeros((B, B), F32)


def first_kernel(table, given, out_ref, k_ref, s_ref, d_ref, u_ref, left_ref, right_ref, f_ref, f3_ref, y_ref):
    lines = given[2 * B :, : 2 * B]
    ends = given[2 * B :, 2 * B :]
    wanted = ends[1:2].astype(jnp.int32)
    tile_hot = (iota((B, COARSE), 0) == wanted // CP).astype(BF16)
    rows = picked(table[:, : 4 * CP], tile_hot, tn)
    rows = jnp.where((iota((4 * CP, COARSE), 0) % CP) == wanted % CP, rows, 0.0)
    across = []
    for k in range(4):
        line = jnp.sum(rows[k * CP : (k + 1) * CP], axis=0, keepdims=True) / ends[2 + k : 3 + k]
        across.append(jnp.concatenate([lines[k : k + 1, :B], line, lines[k : k + 1, B:]], axis=1))
    live = jnp.concatenate([lines[4:5, :B], jnp.ones((1, N - B), F32)], axis=1)
    down = jnp.concatenate(across + [live] + [jnp.zeros((B - 5, N), F32)], axis=0).T
    variance = jnp.concatenate([ends[6:7], ends[6:7, : N - COARSE]], axis=1)
    nugget = jnp.concatenate([ends[7:8], ends[7:8, : N - COARSE]], axis=1)
    for r in range(N // B):
        here = slice(r * B, (r + 1) * B)
        kernel, common, squares = pair(down[here], across, variance, down[here, 4:5], live)
        for i, part in enumerate([common * square for square in squares]):
            there = slice(i * N, (i + 1) * N)
            f_ref[here, there], f_ref[N + r * B : N + (r + 1) * B, there], f3_ref[here, there] = thirds(part)
        same = iota((B, N), 0) + r * B == iota((B, N), 1)
        k_ref[here, :] = kernel + jnp.where(same, live * nugget + 1.0 - live, 0.0)

    def conditional(p):
        at = pl.multiple_of(p * B, B)
        after = pl.multiple_of(p * B + B, B)
        u = nn(six_left(d_ref[...]), six_right(k_ref[pl.ds(at, B), pl.ds(after, B)]), None)
        s_ref[...] = k_ref[pl.ds(after, B), pl.ds(after, B)] - nn(six_left(u.T), six_right(u), None)

    d_ref[...] = given[:B, LEAD:]
    conditional(0)

    def sweep(p, carry):
        tiles = inverse_factor([s_ref[8 * v : 8 * (v + 1), :] for v in range(B // 8)])
        last = pl.multiple_of(p * B - B, B)
        d = d_ref[...]
        u_ref[...] = nn(six_left(d), six_right(k_ref[pl.ds(last, B), :]), None)
        u_ref[:, pl.ds(last, B)] = -d
        k_ref[pl.ds(last, B), :] = jnp.zeros((B, N), F32)
        k_ref[:, pl.ds(last, B)] = jnp.zeros((N, B), F32)
        left_ref[...] = six_left(u_ref[...].T)
        right_ref[...] = six_right(u_ref[...])
        k_ref[...] -= nn(left_ref[...], right_ref[...], None)
        for v in range(B // 8):
            d_ref[8 * v : 8 * (v + 1), :] = tiles[v]

        @pl.when(p < N // B - 1)
        def _():
            conditional(p)

        return carry

    lax.fori_loop(1, N // B, sweep, 0)
    d = d_ref[...]
    out_ref[MROW : MROW + B, :LEAD] = -nt(d, k_ref[:LEAD, LEAD:])
    out_ref[MROW : MROW + B, LEAD:] = d
    m = out_ref[MROW : MROW + B, :]
    parts = halves(m)
    twice = jnp.concatenate([jnp.concatenate([part, part], axis=1) for part in parts], axis=0)
    large = nn(twice, f_ref[...], None)
    small = large[B:] + nn(parts[0], f3_ref[...], None)
    y_ref[:B, :] = m * (live * nugget)
    for i in range(4):
        there = slice(i * N, (i + 1) * N)
        y_ref[(i + 1) * B : (i + 2) * B, :] = large[:B, there] + small[:, there]
    high, low = halves(y_ref[...])
    out_ref[:MROW, :LEAD] = -three_terms((high[:, :LEAD], low[:, :LEAD]), halves(k_ref[:LEAD, :LEAD]), nn)
    out_ref[:MROW, LEAD:] = three_terms((high, low), parts, nt)

    def folded(x):
        x = jnp.sum(x.reshape(B // 8, 8, x.shape[1]), axis=0)
        total = x[:, :B]
        for c in range(1, x.shape[1] // B):
            total = total + x[:, c * B : (c + 1) * B]
        return total

    def z_of(i):
        return out_ref[i * B : (i + 1) * B, :LEAD]

    def g_of(i):
        return out_ref[i * B : (i + 1) * B, LEAD:]

    def line(x):
        return jnp.sum(x, axis=0, keepdims=True)

    eye = (iota((B, B), 0) == iota((B, B), 1)).astype(F32)
    pairs, traces = {}, [line(folded(g_of(i) * eye)) for i in range(5)]
    for i in range(5):
        for j in range(i + 1):
            lead_part = z_of(i) * y_ref[j * B : (j + 1) * B, :LEAD]
            pairs[i, j] = line(2.0 * folded(lead_part) + folded(g_of(i) * g_of(j)))
    ones = jnp.ones((1, B), F32)
    sums = [pairs[0, 0] + (ones - 2.0 * traces[0])]
    for i in range(1, 5):
        sums += [traces[i] - pairs[i, 0]] + [pairs[i, j] for j in range(1, i + 1)]
    sums += [traces[0] - pairs[0, 0]] + [pairs[j, 0] for j in range(1, 5)] + [pairs[0, 0]]
    sums += [ones - traces[0]] + traces[1:] + [traces[0]]
    sums.append(jnp.zeros((B - 27, B), F32))
    out_ref[PROW:, :B] = jnp.broadcast_to(line(jnp.concatenate(sums, axis=0).T), (8, B))


def picked2(one_hot, table):
    high, low = halves(table)
    return nt(one_hot, high, None) + nt(one_hot, low, None)


def second_kernel(arrived, given, fine, white_ref, row_ref, v1_ref, v2_ref):
    reps = white_ref.shape[0]
    chunks = reps // B
    held = arrived.shape[0] // chunks
    v1_ref[:B, :], v2_ref[:B, :] = halves(fine[:B, :reps])
    v1_ref[LEAD:, :], v2_ref[LEAD:, :] = halves(fine[B : 2 * B, :reps])
    place = jnp.broadcast_to(fine[2 * B : 2 * B + 1, 2 * B :], (B, COARSE)).T[:, :1]
    hot = (place == iota((COARSE, held), 1).astype(F32)).astype(BF16)
    for c in range(chunks):
        high, low = halves(arrived[pl.ds(c, held, stride=chunks), :])
        v1_ref[B:LEAD, c * B : (c + 1) * B] = nn(hot, high, None).astype(BF16)
        v2_ref[B:LEAD, c * B : (c + 1) * B] = nn(hot, low, None).astype(BF16)
    parts = thirds(given[MROW : MROW + B, :])
    first = nn(jnp.concatenate(parts, axis=0), v1_ref[...], None)
    second = nn(jnp.concatenate(parts[:2], axis=0), v2_ref[...], None)
    white = first[:B] + ((first[B : 2 * B] + second[:B]) + (first[2 * B :] + second[B:]))
    white_ref[...] = white.T
    split = halves(white)
    cross = three_terms(split, (v1_ref[:LEAD, :], v2_ref[:LEAD, :]), nt)
    square = three_terms(split, split, nt)
    eye = (iota((B, B), 0) == iota((B, B), 1)).astype(F32)
    leads, owns = [], []
    for i in range(5):
        both = given[i * B : (i + 1) * B, :LEAD] * cross
        leads.append((both[:, :B] + both[:, B : 2 * B]) + (both[:, 2 * B : 3 * B] + both[:, 3 * B :]))
        owns.append(0.5 * (given[i * B : (i + 1) * B, LEAD:] * square))
    terms = [0.5 * (eye * square) - owns[0] - leads[0]] + [leads[i] + owns[i] for i in (1, 2, 3, 4, 0)]
    terms = [jnp.sum(term, axis=0, keepdims=True) for term in terms]
    whole = jnp.concatenate([jnp.zeros((21, B), F32)] + terms + [jnp.zeros((B - 27, B), F32)], axis=0)
    weight = jnp.where(iota((1, B), 1) < 21, 0.5 * reps, -0.5 * reps)
    row = jnp.sum(whole.T, axis=0, keepdims=True) + weight * given[PROW : PROW + 1, :B]
    row_ref[...] = jnp.broadcast_to(row, row_ref.shape)


def third_kernel(rows, step_ref):
    total = jnp.broadcast_to(jnp.sum(rows[...], axis=0, keepdims=True), (8, B))
    sub, lane = iota((8, B), 0), iota((8, B), 1)
    a = jnp.zeros((8, B), F32)
    for i in range(6):
        for j in range(6):
            low, high = min(i, j), max(i, j)
            entry = jnp.broadcast_to(total[:, high * (high + 1) // 2 + low : high * (high + 1) // 2 + low + 1], (8, B))
            a = jnp.where((sub == i) & (lane == j), entry, a)
        entry = jnp.broadcast_to(total[:, 21 + i : 22 + i], (8, B))
        a = jnp.where((sub == i) & (lane == 6), entry, a)
    for k in range(6):
        row = jnp.broadcast_to(a[k : k + 1, :], (8, B))
        col = jnp.broadcast_to(a[:, k : k + 1], (8, B))
        row = row / jnp.broadcast_to(row[:, k : k + 1], (8, B))
        a = jnp.where(sub == k, row, a - col * row)
    step_ref[...] = jnp.sum(jnp.where((lane == sub) & (sub < 6), jnp.broadcast_to(a[:, 6:7], (8, B)), 0.0), axis=0)[:6]


def body(coords, values, coarse_coords, coarse_values, fine_index, coarse_index, log_params):
    reps = values.shape[0]
    devices = lax.axis_size("row") * lax.axis_size("col")
    vmem = pl.BlockSpec(memory_space=pltpu.VMEM)
    smem = pl.BlockSpec(memory_space=pltpu.SMEM)

    def shape(*dims):
        return jax.ShapeDtypeStruct(dims, F32)

    def cost(flops):
        return pl.CostEstimate(flops=flops, bytes_accessed=2**20, transcendentals=0)

    def room(mib):
        return pltpu.CompilerParams(vmem_limit_bytes=mib * 2**20)

    request, tile = pl.pallas_call(
        request_kernel,
        out_shape=(shape(devices, B), shape(reps + TAIL, B)),
        in_specs=[smem] + [vmem] * 5,
        out_specs=(vmem,) * 2,
        compiler_params=room(60),
        name="request_part",
    )(log_params, coarse_coords, coarse_index, coords, values, fine_index)
    up = shifted(tile, "row", 1)
    left = passed_along(tile, "col", 1)
    table = lax.all_to_all(request, AXES, 0, 0, tiled=True)
    fine = pl.pallas_call(
        fine_kernel,
        out_shape=shape(2 * B + 8, N),
        in_specs=[vmem] * 3,
        out_specs=vmem,
        compiler_params=room(8),
        cost_estimate=cost(4 * 10**9),
        name="fine_part",
    )(tile, up, left)
    send = pl.pallas_call(
        send_kernel,
        out_shape=shape(devices * MOST * reps // B, B),
        in_specs=[vmem] * 2 + [pl.BlockSpec(memory_space=pl.ANY)],
        out_specs=vmem,
        compiler_params=room(8),
        name="send_part",
    )(table, coarse_values.T, fine)
    arrived = lax.all_to_all(send, AXES, 0, 0, tiled=True)
    parts = pl.pallas_call(
        first_kernel,
        out_shape=shape(TOTAL_ROWS, N),
        in_specs=[vmem] * 2,
        out_specs=vmem,
        scratch_shapes=[
            pltpu.VMEM((N, N), F32),
            pltpu.VMEM((B, B), F32),
            pltpu.VMEM((B, B), F32),
            pltpu.VMEM((B, N), F32),
            pltpu.VMEM((N, 6 * B), BF16),
            pltpu.VMEM((6 * B, N), BF16),
            pltpu.VMEM((2 * N, 4 * N), BF16),
            pltpu.VMEM((N, 4 * N), BF16),
            pltpu.VMEM((5 * B, N), F32),
        ],
        compiler_params=room(36),
        cost_estimate=cost(30 * 10**9),
        name="fisher_part",
    )(table, fine)
    white, row = pl.pallas_call(
        second_kernel,
        out_shape=(shape(reps, B), shape(devices, B)),
        in_specs=[vmem] * 3,
        out_specs=(vmem,) * 2,
        scratch_shapes=[pltpu.VMEM((N, reps), BF16), pltpu.VMEM((N, reps), BF16)],
        compiler_params=room(24),
        name="gradient_part",
    )(arrived, parts, fine)
    rows = lax.all_to_all(row, AXES, 0, 0, tiled=True)
    step = pl.pallas_call(
        third_kernel,
        out_shape=shape(6),
        in_specs=[vmem],
        out_specs=vmem,
        compiler_params=room(8),
        name="solve_part",
    )(rows)
    return (step, white)


def solution(mesh):
    in_specs = (
        P(None, AXES),
        P(None, AXES),
        P(None, AXES),
        P(None, AXES),
        P(AXES, None),
        P(AXES, None),
        P(),
    )
    out_specs = (P(), P(None, AXES))
    return jax.shard_map(body, mesh=mesh, in_specs=in_specs, out_specs=out_specs, check_vma=False)
```
